32 devices in a mesh: mem: 4 (over y, x), grid: 8 (over z, core).
Axes of the slice: x: 2, y: 2, z: 4, core: 2. Of those that a mesh axis runs over, the one named last changes fastest.
Arguments:
- ensemble: bfloat16 [1024, 128, 1024], P(('mem', 'grid')), may hold values from -6 to 6
- right_side: float32 [128, 1024], P(('mem', 'grid')), may hold values from -18 to 18
- obs_prec: float32 [128, 1024], P(('mem', 'grid')), may hold values from 0.5 to 2
- neighbors: int32 [128, 8], replicated, may hold values from 0 to 127, as said below
- loc_weight: float32 [128, 8], replicated, may hold values from 0 to 0.08
Outputs:
- solution_field: float32 [128, 1024], P(('mem', 'grid'))
- residual: float32 [128, 1024], P(('mem', 'grid'))
The draws below stay inside these ranges and needn't reach their ends.
Inputs may be any that keep to these rules, and one draw needn't show every extreme that they name: neighbors[b, j] lies within 3 of b along the cyclic order of blocks, and every block is listed exactly once in each of the 8 columns.
All inputs are finite; a program needn't handle non-finite values.
Results may differ from the reference program's by a relative error of at most 0.0073.
Values may be sent and summed in bfloat16 or wider, within the bound.
No kernel may reach another device: no remote copies, remote signals or barrier semaphores. Data moves between devices by JAX's collectives and lax.ppermute only.
A program may use at most 128 MiB of HBM per device.

```python
import math
import jax
import jax.numpy as jnp
from jax import lax

M = 1024
NB = 8
ITERS = 2
BLK_DEV = 4
CELL = 1024
NBLK = 128


def draw_right_side(key, part):
    rows = jnp.arange(NBLK, dtype=jnp.float32)[:, None]
    base = jax.random.truncated_normal(key, -6.0, 6.0, (NBLK, CELL), jnp.float32)
    return base * (1.0 + 2.0 * rows / NBLK)


def draw_neighbors(key, part):
    windows = NBLK // BLK_DEV
    columns = []
    for slot in range(NB):
        offset = slot * BLK_DEV // NB
        keys = jax.random.split(jax.random.fold_in(key, slot + 11), windows)
        perms = jax.vmap(lambda k: jax.random.permutation(k, BLK_DEV))(keys).astype(jnp.int32)
        starts = jnp.arange(windows, dtype=jnp.int32)[:, None] * BLK_DEV + offset
        source = (starts + jnp.arange(BLK_DEV, dtype=jnp.int32)[None, :]) % NBLK
        target = (starts + perms) % NBLK
        column = jnp.zeros((NBLK,), jnp.int32).at[source.reshape(-1)].set(target.reshape(-1))
        columns.append(column)
    return jnp.stack(columns, axis=1)


def block_levels(key, shape, shards, low, high):
    factor_of, own = 1.0, jax.random.fold_in(key, 6)
    for position, blocks in shards:
        draws = jnp.exp(jax.random.uniform(jax.random.fold_in(own, position), (blocks,), jnp.float32, low / len(shards), high / len(shards)))
        factor_of = factor_of * jnp.repeat(draws, shape[position] // blocks).reshape([-1 if axis == position else 1 for axis in range(len(shape))])
    return factor_of


def bell_draw(stream_key, dims, scale, limit, cuts=(), held_as=jnp.bfloat16):
    result = jax.random.normal(stream_key, dims, jnp.float32) * scale
    if len(cuts) > 0:
        result = block_levels(stream_key, dims, cuts, -0.22, 0.18) * result
    return jnp.clip(result, min=-limit, max=limit).astype(held_as)


def setup_inputs(seed: int = 0) -> dict:
    splits = jax.random.split(jax.random.key(seed), 6)
    ensemble = bell_draw(splits[0], (M, NBLK, CELL), 1.0, 6.0, ((0, 32),))
    right_side = draw_right_side(jax.random.fold_in(splits[5], 71), 0)
    obs_prec = jnp.clip(0.5 + 1.5 * jax.random.uniform(splits[2], (NBLK, CELL), jnp.float32) ** block_levels(splits[2], (NBLK, CELL), ((0, 32),), -0.2, 0.2), 0.5, 2.0)
    neighbors = draw_neighbors(jax.random.fold_in(splits[5], 71), 0)
    loc_weight = jnp.clip(jax.random.uniform(splits[4], (NBLK, NB), jnp.float32, 0.0, 0.08), 0.0, 0.08)
    return {"ensemble": ensemble, "right_side": right_side, "obs_prec": obs_prec, "neighbors": neighbors, "loc_weight": loc_weight}


def apply_operator(direction, ensemble, obs_prec, neighbors, loc_weight):
    group = math.gcd(NBLK, 32)
    count = NBLK // group
    rounded = direction.astype(jnp.bfloat16)

    def sums_of(k):
        part = lax.dynamic_slice_in_dim(ensemble, k * group, group, 1).astype(jnp.float32)
        dpart = lax.dynamic_slice_in_dim(rounded, k * group, group, 0).astype(jnp.float32)
        return jnp.einsum('mbc,bc->bm', part, dpart)

    block_sum = lax.map(sums_of, jnp.arange(count, dtype=jnp.int32)).reshape(NBLK, M)
    picked = jnp.take(block_sum, neighbors, axis=0)
    coeff = (block_sum + jnp.sum(picked * loc_weight[:, :, None], axis=1)).astype(jnp.bfloat16)

    def spread_of(k):
        part = lax.dynamic_slice_in_dim(ensemble, k * group, group, 1).astype(jnp.float32)
        cpart = lax.dynamic_slice_in_dim(coeff, k * group, group, 0).astype(jnp.float32)
        return jnp.einsum('mbc,bm->bc', part, cpart)

    spread = lax.map(spread_of, jnp.arange(count, dtype=jnp.int32)).reshape(NBLK, CELL)
    return obs_prec * direction + spread * (1.0 / M)


def reference(ensemble, right_side, obs_prec, neighbors, loc_weight):
    solution_field = jnp.zeros_like(right_side)
    residual = right_side
    direction = right_side
    norm_now = jnp.sum(residual * residual)
    for step in range(ITERS):
        image = apply_operator(direction, ensemble, obs_prec, neighbors, loc_weight)
        alpha = norm_now / jnp.sum(direction * image)
        solution_field = solution_field + alpha * direction
        residual = residual - alpha * image
        norm_next = jnp.sum(residual * residual)
        direction = residual + (norm_next / norm_now) * direction
        norm_now = norm_next
    return solution_field, residual
```

```python
import functools

import jax
import jax.numpy as jnp
from jax import lax
from jax.experimental import pallas as pl
from jax.experimental.pallas import tpu as pltpu
from jax.sharding import PartitionSpec as P

AXES = ("mem", "grid")
M = 1024
LANES = 128
KEEP = 0.25
REACH = 3
F32 = jnp.float32
BF16 = jnp.bfloat16
VMEM = pl.BlockSpec(memory_space=pltpu.VMEM)


def halves_of(x):
    blocks, cells = x.shape
    tiles = cells // (2 * LANES)
    return x.reshape(blocks, 2, tiles, LANES).transpose(1, 0, 2, 3).reshape(2, blocks * tiles, LANES)


def whole_of(x, blocks):
    tiles = x.shape[1] // blocks
    return x.reshape(2, blocks, tiles, LANES).transpose(1, 0, 2, 3).reshape(blocks, 2 * tiles * LANES)


def core_index():
    return lax.rem(lax.axis_index("grid"), 2)


def block_sums(ens_ref, fields, sums_ref, rows, tiles):
    members, blocks, cells = ens_ref.shape
    core = core_index()
    lane = lax.broadcasted_iota(jnp.int32, (rows, LANES), 1)

    def group(g, _):
        base = pl.multiple_of(g * rows, rows)
        parts = []
        for slot in range(2):
            col = lax.rem(core + slot, 2) * (cells // 2)
            for t in range(tiles):
                at = pl.ds(g * rows * tiles + t, rows, stride=tiles)
                parts.append((pl.multiple_of(col + t * LANES, LANES), fields[slot][at, :]))
        out = jnp.zeros((rows, LANES), F32)
        for k in range(members):
            acc = None
            for at, part in parts:
                term = ens_ref[k, pl.ds(base, rows), pl.ds(at, LANES)].astype(F32) * part
                acc = term if acc is None else acc + term
            out = jnp.where(lane == k, jnp.sum(acc, axis=1, keepdims=True), out)
        sums_ref[pl.ds(base, rows), :] = out
        return 0

    lax.fori_loop(0, blocks // rows, group, 0)


def mixed(sums, pad_ref, nbr_ref, weight_ref):
    blocks = sums.shape[0]
    pad_ref[pl.ds(8, blocks), :] = sums
    pad_ref[pl.ds(0, 8), :] = sums[blocks - 8 :]
    pad_ref[pl.ds(8 + blocks, 8), :] = sums[:8]
    away = nbr_ref[...] - lax.broadcasted_iota(jnp.int32, nbr_ref.shape, 0)
    away = jnp.where(away > blocks // 2, away - blocks, away)
    away = jnp.where(away < -(blocks // 2), away + blocks, away)
    total = sums
    for step in range(-REACH, REACH + 1):
        share = jnp.sum(jnp.where(away == step, weight_ref[...], 0.0), axis=1, keepdims=True)
        total = total + share * pad_ref[pl.ds(8 + step, blocks), :]
    return total.astype(BF16).astype(F32)


def spreads(ens_ref, coeff_ref, outs, rows, tiles):
    members, blocks, cells = ens_ref.shape
    core = core_index()

    def group(g, _):
        base = pl.multiple_of(g * rows, rows)
        coeff = coeff_ref[pl.ds(base, rows), :]
        acc = [None] * (2 * tiles)
        for k in range(members):
            one = jnp.broadcast_to(coeff[:, k : k + 1], (rows, LANES))
            for slot in range(2):
                col = lax.rem(core + slot, 2) * (cells // 2)
                for t in range(tiles):
                    at = pl.multiple_of(col + t * LANES, LANES)
                    term = ens_ref[k, pl.ds(base, rows), pl.ds(at, LANES)].astype(F32) * one
                    i = slot * tiles + t
                    acc[i] = term if acc[i] is None else acc[i] + term
        for slot in range(2):
            for t in range(tiles):
                outs[slot][pl.ds(g * rows * tiles + t, rows, stride=tiles), :] = acc[slot * tiles + t]
        return 0

    lax.fori_loop(0, blocks // rows, group, 0)


def by_block(x, blocks):
    tiles = x.shape[0] // blocks
    return jnp.sum(x, axis=1, keepdims=True).reshape(blocks, tiles)


def first_kernel(tiles, ens_ref, mine_ref, other_ref, nbr_ref, weight_ref, own_ref, send_ref, sums_ref, fields, pad_ref, coeff_ref):
    fields[0] = mine_ref[...].astype(F32)
    fields[1] = other_ref[...].astype(F32)
    block_sums(ens_ref, (fields.at[0], fields.at[1]), sums_ref, 16, tiles)
    coeff_ref[...] = mixed(sums_ref[...], pad_ref, nbr_ref, weight_ref)
    spreads(ens_ref, coeff_ref, (own_ref, send_ref), 16, tiles)


def second_kernel(
    tiles, ens_ref, dm_ref, do_ref, pm_ref, po_ref, nbr_ref, weight_ref, sums0_ref, d_own_ref, q_own_ref, obs_ref,
    own_ref, send_ref, scal_ref, fields, sums_ref, pad_ref, coeff_ref,
):
    blocks = ens_ref.shape[1]
    fields[0] = pm_ref[...].astype(F32)
    fields[1] = po_ref[...].astype(F32)
    block_sums(ens_ref, (fields.at[0], fields.at[1]), sums_ref, 16, tiles)
    prod = jnp.zeros((blocks, LANES), F32)
    self = jnp.zeros((blocks, LANES), F32)
    dirs = []
    gots = []
    fields[2] = dm_ref[...].astype(F32)
    fields[3] = do_ref[...].astype(F32)
    for slot in range(2):
        for t in range(tiles):
            d = fields[2 + slot, pl.ds(t, blocks, stride=tiles), :]
            p = fields[slot, pl.ds(t, blocks, stride=tiles), :]
            prod = prod + d * p
            self = self + d * d
    pd = jnp.sum(prod, axis=1, keepdims=True)
    dd = jnp.sum(self, axis=1, keepdims=True)
    tau = jnp.where(dd > 0.0, (1.0 / KEEP - 1.0) * pd / jnp.where(dd > 0.0, dd, 1.0), 0.0)
    rr0 = jnp.sum(dd)
    alpha = rr0 / jnp.sum(pd + tau * dd)
    keep = 1.0 - alpha * tau
    left = jnp.zeros((blocks, LANES), F32)
    for slot in range(2):
        for t in range(tiles):
            d = fields[2 + slot, pl.ds(t, blocks, stride=tiles), :]
            p = fields[slot, pl.ds(t, blocks, stride=tiles), :]
            r = keep * d - alpha * p
            left = left + r * r
    rr1 = jnp.sum(left)
    beta = rr1 / rr0
    sums = (beta + keep) * sums0_ref[...] - alpha * sums_ref[...]
    coeff = mixed(sums, pad_ref, nbr_ref, weight_ref)
    coeff_ref[...] = coeff
    direction = (1.0 + beta) * d_own_ref[...] - alpha * q_own_ref[...]
    part = jnp.sum(sums * coeff) * (1.0 / M) + jnp.sum(obs_ref[...] * direction * direction)
    row = lax.broadcasted_iota(jnp.int32, (8, LANES), 0)
    scal_ref[...] = jnp.where(row == 0, part, jnp.where(row == 1, alpha, jnp.where(row == 2, beta, rr1)))
    spreads(ens_ref, coeff_ref, (own_ref, send_ref), 16, tiles)


def params():
    return pltpu.CompilerParams(vmem_limit_bytes=40 * 1024 * 1024)


def per_device(ensemble, right_side, obs_prec, neighbors, loc_weight):
    own, cells = right_side.shape
    members, blocks, _ = ensemble.shape
    devices = lax.axis_size(AXES)
    tiles = cells // (2 * LANES)
    rows = own * tiles
    pairs = [(i, i ^ 1) for i in range(devices)]
    direct = halves_of(right_side)
    obs = halves_of(obs_prec)

    def gathered(x):
        sent = jnp.broadcast_to(x[None], (devices // 2, 2, rows, LANES)).reshape(devices, rows, LANES)
        mine = lax.all_to_all(sent, AXES, split_axis=0, concat_axis=0, tiled=True).reshape(devices * rows, LANES)
        return mine, lax.ppermute(mine, AXES, pairs)

    def scattered(mine, send):
        both = (mine + lax.ppermute(send, AXES, pairs)).astype(BF16).reshape(devices, rows, LANES)
        return both

    half = jax.ShapeDtypeStruct((blocks * tiles, LANES), F32)
    table = jax.ShapeDtypeStruct((blocks, LANES), F32)
    fields = pltpu.VMEM((2, blocks * tiles, LANES), F32)
    padded = pltpu.VMEM((blocks + 16, LANES), F32)
    coeffs = pltpu.VMEM((blocks, LANES), F32)

    d_mine, d_other = gathered(direct.astype(BF16))
    mine, send, sums0 = pl.pallas_call(
        functools.partial(first_kernel, tiles),
        out_shape=(half, half, table),
        in_specs=[VMEM] * 5,
        out_specs=(VMEM, VMEM, VMEM),
        scratch_shapes=[fields, padded, coeffs],
        compiler_params=params(),
    )(ensemble, d_mine, d_other, neighbors, loc_weight)
    got = lax.all_to_all(scattered(mine, send), AXES, split_axis=0, concat_axis=0, tiled=True)
    spread = jnp.sum(got.reshape(devices // 2, 2, rows, LANES).astype(F32), axis=0)
    q = obs * direct + spread * (1.0 / M)

    d16 = direct.astype(BF16).astype(F32).reshape(2, own, tiles, LANES)
    dd = jnp.sum(d16 * d16, axis=(0, 2, 3), keepdims=True)
    qd = jnp.sum(d16 * q.reshape(d16.shape), axis=(0, 2, 3), keepdims=True)
    tau = jnp.where(dd > 0.0, (1.0 - KEEP) * qd / jnp.where(dd > 0.0, dd, 1.0), 0.0)
    p = (q.reshape(d16.shape) - tau * d16).reshape(q.shape).astype(BF16)
    p_mine, p_other = gathered(p)
    mine, send, scal = pl.pallas_call(
        functools.partial(second_kernel, tiles),
        out_shape=(half, half, jax.ShapeDtypeStruct((8, LANES), F32)),
        in_specs=[VMEM] * 11,
        out_specs=(VMEM, VMEM, VMEM),
        scratch_shapes=[pltpu.VMEM((4, blocks * tiles, LANES), F32), coeffs, padded, coeffs],
        compiler_params=params(),
    )(ensemble, d_mine, d_other, p_mine, p_other, neighbors, loc_weight, sums0, direct, q, obs)
    part, alpha, beta, rr1 = (scal[0, 0], scal[1, 0], scal[2, 0], scal[3, 0])
    high = part.astype(BF16)
    rest = part - high.astype(F32)
    middle = rest.astype(BF16)
    low = (rest - middle.astype(F32)).astype(BF16)
    extra = jnp.broadcast_to(jnp.stack([high, middle, low] + [jnp.zeros_like(low)] * 5)[None, :, None], (devices, 8, LANES))
    sent = jnp.concatenate([scattered(mine, send), extra], axis=1)
    got = lax.all_to_all(sent, AXES, split_axis=0, concat_axis=0, tiled=True).astype(F32)
    spread = jnp.sum(got[:, :rows].reshape(devices // 2, 2, rows, LANES), axis=0)
    denom = jnp.sum(got[:, rows:, 0])
    residual = direct - alpha * q
    direction = residual + beta * direct
    image = obs * direction + spread * (1.0 / M)
    alpha1 = rr1 / denom
    solution_field = alpha * direct + alpha1 * direction
    residual = residual - alpha1 * image
    return whole_of(solution_field, own), whole_of(residual, own)


def solution(mesh):
    return jax.shard_map(
        per_device,
        mesh=mesh,
        in_specs=(
            P(AXES, None, None),
            P(AXES, None),
            P(AXES, None),
            P(),
            P(),
        ),
        out_specs=(P(AXES, None), P(AXES, None)),
        check_vma=False,
    )
```

```python
import functools

import jax
import jax.numpy as jnp
from jax import lax
from jax.experimental import pallas as pl
from jax.experimental.pallas import tpu as pltpu
from jax.sharding import PartitionSpec as P

AXES = ("mem", "grid")
M = 1024
LANES = 128
ROWS = 16
KEEP = 0.25
REACH = 3
SHIFTS = range(-REACH, REACH + 1)
F32 = jnp.float32
BF16 = jnp.bfloat16
VMEM = pl.BlockSpec(memory_space=pltpu.VMEM)
HBM = pl.BlockSpec(memory_space=pltpu.HBM)


def core_index():
    return lax.rem(lax.axis_index("grid"), 2)


def every(ref, t, first, blocks, tiles):
    return ref[pl.ds(first * tiles + t, blocks, stride=tiles), :]


def lay_kernel(tiles, field_ref, halves_ref):
    own = field_ref.shape[0]
    for h in range(2):
        for t in range(tiles):
            cells = pl.ds((h * tiles + t) * LANES, LANES)
            halves_ref[pl.ds(h * own * tiles + t, own, stride=tiles), :] = field_ref[:, cells]


def start_kernel(tiles, right_ref, sent_ref, direct_ref):
    lay_kernel(tiles, right_ref, direct_ref)
    spread_out(direct_ref[...].astype(BF16), sent_ref)


def spread_out(both, sent_ref):
    devices, rows, _ = sent_ref.shape
    low, high = both[:rows], both[rows:]
    for chip in range(devices // 2):
        sent_ref[2 * chip] = low
        sent_ref[2 * chip + 1] = high


def load_kernel(
    tiles, ens_hbm, nbr_hbm, weight_hbm, obs_hbm, mine_ref, ens_ref, share_ref, acc_ref, obs_ref,
    held, mine, nbr_ref, weight_ref, laid, sems, small,
):
    members, blocks, cells = ens_hbm.shape
    half = cells // 2
    core = core_index()
    groups = blocks // ROWS

    def copies(g):
        span = pl.ds(pl.multiple_of(g * ROWS, ROWS), ROWS)
        out = []
        for slot in range(2):
            col = pl.multiple_of(lax.rem(core + slot, 2) * half, half)
            source = ens_hbm.at[:, span, pl.ds(col, half)]
            out.append(pltpu.make_async_copy(source, held.at[slot, :, span], sems.at[slot, g]))
        return out

    lists = (
        pltpu.make_async_copy(nbr_hbm, nbr_ref, small.at[0]),
        pltpu.make_async_copy(weight_hbm, weight_ref, small.at[1]),
        pltpu.make_async_copy(obs_hbm, laid, small.at[2]),
    )
    for copy in lists:
        copy.start()

    def begin(g, _):
        for copy in copies(g):
            copy.start()
        return 0

    lax.fori_loop(0, groups, begin, 0)
    mine[...] = mine_ref[...].astype(F32)
    for copy in lists:
        copy.wait()
    lay_kernel(tiles, laid, obs_ref)
    away = nbr_ref[...] - lax.broadcasted_iota(jnp.int32, nbr_ref.shape, 1)
    away = jnp.where(away > blocks // 2, away - blocks, away)
    away = jnp.where(away < -(blocks // 2), away + blocks, away)
    row = lax.broadcasted_iota(jnp.int32, (8, blocks), 0)
    shares = jnp.zeros((8, blocks), F32)
    for i, shift in enumerate(SHIFTS):
        share = jnp.sum(jnp.where(away == shift, weight_ref[...], 0.0), axis=0, keepdims=True)
        shares = jnp.where(row == i, share, shares)
    shares = shares.T
    for i in range(len(SHIFTS)):
        share_ref[i] = jnp.broadcast_to(shares[:, i : i + 1], (blocks, LANES))

    def group(g, _):
        first = pl.multiple_of(g * ROWS, ROWS)
        for copy in copies(g):
            copy.wait()
        parts = [every(mine, t, first, ROWS, tiles) for t in range(tiles)]
        for k in range(members):
            acc = None
            for t in range(tiles):
                cells = pl.ds(t * LANES, LANES)
                one = held[0, k, pl.ds(first, ROWS), cells].astype(F32)
                ens_ref[0, k, pl.ds(first, ROWS), cells] = one
                acc = one * parts[t] if acc is None else acc + one * parts[t]
            acc_ref[k, pl.ds(first, ROWS), :] = acc
            for t in range(tiles):
                cells = pl.ds(t * LANES, LANES)
                ens_ref[1, k, pl.ds(first, ROWS), cells] = held[1, k, pl.ds(first, ROWS), cells].astype(F32)
        return 0

    lax.fori_loop(0, groups, group, 0)


def own_sums_kernel(tiles, ens_ref, mine_ref, acc_ref, mine):
    _, members, blocks, _ = ens_ref.shape
    mine[...] = mine_ref[...].astype(F32)

    def group(g, _):
        first = pl.multiple_of(g * ROWS, ROWS)
        parts = [every(mine, t, first, ROWS, tiles) for t in range(tiles)]
        for k in range(members):
            acc = None
            for t in range(tiles):
                term = ens_ref[0, k, pl.ds(first, ROWS), pl.ds(t * LANES, LANES)] * parts[t]
                acc = term if acc is None else acc + term
            acc_ref[k, pl.ds(first, ROWS), :] = acc
        return 0

    lax.fori_loop(0, blocks // ROWS, group, 0)


def block_sums(ens_ref, acc_ref, field, sums_ref, tiles):
    _, members, blocks, _ = ens_ref.shape
    lane = lax.broadcasted_iota(jnp.int32, (ROWS, LANES), 1)

    def group(g, _):
        first = pl.multiple_of(g * ROWS, ROWS)
        parts = [every(field, t, first, ROWS, tiles) for t in range(tiles)]
        out = jnp.zeros((ROWS, LANES), F32)
        for k in range(members):
            acc = acc_ref[k, pl.ds(first, ROWS), :]
            for t in range(tiles):
                acc = acc + ens_ref[1, k, pl.ds(first, ROWS), pl.ds(t * LANES, LANES)] * parts[t]
            out = jnp.where(lane == k, jnp.sum(acc, axis=1, keepdims=True), out)
        sums_ref[pl.ds(first, ROWS), :] = out
        return 0

    lax.fori_loop(0, blocks // ROWS, group, 0)


def mixed(sums, pad_ref, share_ref):
    blocks = sums.shape[0]
    pad_ref[pl.ds(8, blocks), :] = sums
    pad_ref[pl.ds(0, 8), :] = sums[blocks - 8 :]
    pad_ref[pl.ds(8 + blocks, 8), :] = sums[:8]
    total = sums
    for i, shift in enumerate(SHIFTS):
        total = total + share_ref[i] * pad_ref[pl.ds(8 + shift, blocks), :]
    return total.astype(BF16).astype(F32)


def half_spread(ens_ref, slot, coeff, wide_ref, out_ref, tiles):
    _, members, blocks, _ = ens_ref.shape

    def group(g, _):
        first = pl.multiple_of(g * ROWS, ROWS)
        here = None if coeff is None else coeff[pl.ds(first, ROWS), :]
        acc = [None] * tiles
        for k in range(members):
            if here is None:
                one = wide_ref[k, pl.ds(first, ROWS), :]
            else:
                one = jnp.broadcast_to(here[:, k : k + 1], (ROWS, LANES))
                wide_ref[k, pl.ds(first, ROWS), :] = one
            for t in range(tiles):
                term = ens_ref[slot, k, pl.ds(first, ROWS), pl.ds(t * LANES, LANES)] * one
                acc[t] = term if acc[t] is None else acc[t] + term
        for t in range(tiles):
            out_ref[pl.ds(first * tiles + t, ROWS, stride=tiles), :] = acc[t]
        return 0

    lax.fori_loop(0, blocks // ROWS, group, 0)


def first_kernel(tiles, ens_ref, acc_ref, other_ref, share_ref, send_ref, sums_ref, wide_ref, other, pad_ref, coeff_ref):
    other[...] = other_ref[...].astype(F32)
    block_sums(ens_ref, acc_ref, other, sums_ref, tiles)
    coeff_ref[...] = mixed(sums_ref[...], pad_ref, share_ref)
    half_spread(ens_ref, 1, coeff_ref, wide_ref, send_ref, tiles)


def own_kernel(tiles, ens_ref, wide_ref, own_ref):
    half_spread(ens_ref, 0, None, wide_ref, own_ref, tiles)


def received(got, rows):
    devices = got.shape[0]
    sums = []
    for core in range(2):
        total = None
        for chip in range(devices // 2):
            one = got[2 * chip + core, :rows, :].astype(F32)
            total = one if total is None else total + one
        sums.append(total)
    return jnp.concatenate(sums, axis=0)


def middle_kernel(tiles, got_ref, direct_ref, obs_ref, q_ref, sent_ref):
    _, rows, _ = got_ref.shape
    direct = direct_ref[...]
    q = obs_ref[...] * direct + received(got_ref, rows) * (1.0 / M)
    q_ref[...] = q
    d = direct.astype(BF16).astype(F32)
    dd = jnp.sum(d * d, axis=1, keepdims=True)
    qd = jnp.sum(d * q, axis=1, keepdims=True)
    row = lax.broadcasted_iota(jnp.int32, dd.shape, 0) % rows // tiles
    tau = jnp.zeros_like(dd)
    for b in range(rows // tiles):
        here = row == b
        self = jnp.sum(jnp.where(here, dd, 0.0), axis=0, keepdims=True)
        prod = jnp.sum(jnp.where(here, qd, 0.0), axis=0, keepdims=True)
        share = jnp.where(self > 0.0, (1.0 - KEEP) * prod / jnp.where(self > 0.0, self, 1.0), 0.0)
        tau = jnp.where(here, share, tau)
    spread_out((q - tau * d).astype(BF16), sent_ref)


def second_kernel(
    tiles, ens_ref, acc_ref, dm_ref, do_ref, pm_ref, po_ref, share_ref, sums0_ref, direct_ref, q_ref, obs_ref,
    send_ref, wide_ref, scal_ref, extra_ref, mine, other, dm, do, sums_ref, pad_ref, coeff_ref,
):
    blocks = ens_ref.shape[2]
    mine[...] = pm_ref[...].astype(F32)
    other[...] = po_ref[...].astype(F32)
    dm[...] = dm_ref[...].astype(F32)
    do[...] = do_ref[...].astype(F32)
    block_sums(ens_ref, acc_ref, other, sums_ref, tiles)
    prod = jnp.zeros((blocks, LANES), F32)
    self = jnp.zeros((blocks, LANES), F32)
    halves = ((dm, mine), (do, other))
    for d_ref, p_ref in halves:
        for t in range(tiles):
            d = every(d_ref, t, 0, blocks, tiles)
            prod = prod + d * every(p_ref, t, 0, blocks, tiles)
            self = self + d * d
    pd = jnp.sum(prod, axis=1, keepdims=True)
    dd = jnp.sum(self, axis=1, keepdims=True)
    tau = jnp.where(dd > 0.0, (1.0 / KEEP - 1.0) * pd / jnp.where(dd > 0.0, dd, 1.0), 0.0)
    rr0 = jnp.sum(dd, axis=0, keepdims=True)
    alpha = rr0 / jnp.sum(pd + tau * dd, axis=0, keepdims=True)
    keep = 1.0 - alpha * tau
    left = jnp.zeros((blocks, LANES), F32)
    for d_ref, p_ref in halves:
        for t in range(tiles):
            r = keep * every(d_ref, t, 0, blocks, tiles) - alpha * every(p_ref, t, 0, blocks, tiles)
            left = left + r * r
    rr1 = jnp.sum(jnp.sum(left, axis=1, keepdims=True), axis=0, keepdims=True)
    beta = rr1 / rr0
    sums = (beta + keep) * sums0_ref[...] - alpha * sums_ref[...]
    coeff = mixed(sums, pad_ref, share_ref)
    coeff_ref[...] = coeff
    direction = (1.0 + beta) * direct_ref[...] - alpha * q_ref[...]
    part = jnp.sum(jnp.sum(sums * coeff, axis=0, keepdims=True), axis=1, keepdims=True) * (1.0 / M)
    part += jnp.sum(jnp.sum(obs_ref[...] * direction * direction, axis=0, keepdims=True), axis=1, keepdims=True)
    row = lax.broadcasted_iota(jnp.int32, (8, LANES), 0)
    scal_ref[...] = jnp.where(row == 0, alpha, jnp.where(row == 1, beta, rr1))
    high = part.astype(BF16).astype(F32)
    mid = (part - high).astype(BF16).astype(F32)
    extra_ref[...] = jnp.where(row == 0, high, jnp.where(row == 1, mid, jnp.where(row == 2, part - high - mid, 0.0)))
    half_spread(ens_ref, 1, coeff_ref, wide_ref, send_ref, tiles)


def last_kernel(tiles, got_ref, scal_ref, direct_ref, obs_ref, q_ref, solution_ref, residual_ref, sol, res):
    devices, rows, _ = got_ref.shape
    rows -= 8
    denom = jnp.zeros((8, LANES), F32)
    for i in range(devices):
        denom = denom + got_ref[i, rows:, :].astype(F32)
    denom = jnp.sum(denom, axis=0, keepdims=True)
    alpha, beta, rr1 = scal_ref[0:1, :], scal_ref[1:2, :], scal_ref[2:3, :]
    direct = direct_ref[...]
    residual = direct - alpha * q_ref[...]
    direction = residual + beta * direct
    image = obs_ref[...] * direction + received(got_ref, rows) * (1.0 / M)
    alpha1 = rr1 / denom
    sol[...] = alpha * direct + alpha1 * direction
    res[...] = residual - alpha1 * image
    own = solution_ref.shape[0]
    for h in range(2):
        for t in range(tiles):
            cells = pl.ds((h * tiles + t) * LANES, LANES)
            at = pl.ds(h * rows + t, own, stride=tiles)
            solution_ref[:, cells] = sol[at, :]
            residual_ref[:, cells] = res[at, :]


def call(kernel, name, outs, ins, scratch=(), mib=8, cost=(0, 0)):
    return pl.pallas_call(
        kernel,
        name=name,
        out_shape=tuple(outs),
        in_specs=ins,
        out_specs=(VMEM,) * len(outs),
        scratch_shapes=list(scratch),
        compiler_params=pltpu.CompilerParams(vmem_limit_bytes=mib * 1024 * 1024),
        cost_estimate=pl.CostEstimate(flops=cost[0], bytes_accessed=cost[1], transcendentals=0),
    )


def per_device(ensemble, right_side, obs_prec, neighbors, loc_weight):
    own, cells = right_side.shape
    members, blocks, _ = ensemble.shape
    devices = lax.axis_size(AXES)
    tiles = cells // (2 * LANES)
    rows = own * tiles
    half = blocks * tiles
    pairs = [(i, i ^ 1) for i in range(devices)]
    shape = jax.ShapeDtypeStruct
    part = functools.partial
    mib = 4 + 4 * blocks // 128

    def swap(x):
        return lax.ppermute(x, AXES, pairs)

    def exchange(x):
        return lax.all_to_all(x, AXES, split_axis=0, concat_axis=0, tiled=True)

    to_all = shape((devices, rows, LANES), BF16)
    lanes = shape((members, blocks, LANES), F32)
    table = shape((blocks, LANES), F32)
    part_half = shape((half, LANES), F32)
    mine = shape((2 * rows, LANES), F32)
    field = pltpu.VMEM((half, LANES), F32)
    padded = pltpu.VMEM((blocks + 16, LANES), F32)
    work = 2 * members * blocks * cells

    sent, direct = call(part(start_kernel, tiles), "start", (to_all, mine), [VMEM])(right_side)
    d_mine = exchange(sent).reshape(half, LANES)
    d_other = swap(d_mine)
    ens, share, acc, obs = call(
        part(load_kernel, tiles),
        "load",
        (shape((2, members, blocks, cells // 2), F32), shape((len(SHIFTS), blocks, LANES), F32), lanes, mine),
        [HBM, HBM, HBM, HBM, VMEM],
        [
            pltpu.VMEM((2, members, blocks, cells // 2), BF16),
            field,
            pltpu.VMEM(neighbors.shape[::-1], jnp.int32),
            pltpu.VMEM(loc_weight.shape[::-1], F32),
            pltpu.VMEM((own, cells), F32),
            pltpu.SemaphoreType.DMA((2, blocks // ROWS)),
            pltpu.SemaphoreType.DMA((3,)),
        ],
        mib=8 + mib,
        cost=(work, 6 * members * blocks * cells),
    )(*(pltpu.with_memory_space_constraint(x, pltpu.HBM) for x in (ensemble, neighbors.T, loc_weight.T, obs_prec)), d_mine)

    coeffs = pltpu.VMEM((blocks, LANES), F32)
    send, sums0, wide = call(
        part(first_kernel, tiles), "first", (part_half, table, lanes), [VMEM] * 4, [field, padded, coeffs],
        mib=mib, cost=(work, 0),
    )(ens, acc, d_other, share)
    (kept,) = call(part(own_kernel, tiles), "own", (part_half,), [VMEM] * 2, mib=mib, cost=(work, 0))(ens, wide)
    got = exchange((kept + swap(send)).astype(BF16).reshape(to_all.shape))

    q, sent = call(part(middle_kernel, tiles), "middle", (mine, to_all), [VMEM] * 3)(got, direct, obs)
    p_mine = exchange(sent).reshape(half, LANES)
    p_other = swap(p_mine)

    small = shape((8, LANES), F32)
    (acc,) = call(part(own_sums_kernel, tiles), "sums", (lanes,), [VMEM] * 2, [field], mib=mib, cost=(work, 0))(ens, p_mine)
    send, wide, scal, extra = call(
        part(second_kernel, tiles),
        "second",
        (part_half, lanes, small, small),
        [VMEM] * 11,
        [field] * 4 + [coeffs, padded, coeffs],
        mib=mib, cost=(work, 0),
    )(ens, acc, d_mine, d_other, p_mine, p_other, share, sums0, direct, q, obs)
    (kept,) = call(part(own_kernel, tiles), "own", (part_half,), [VMEM] * 2, mib=mib, cost=(work, 0))(ens, wide)
    both = (kept + swap(send)).reshape(to_all.shape)
    both = jnp.concatenate([both, jnp.broadcast_to(extra[None], (devices, 8, LANES))], axis=1)
    got = exchange(both.astype(BF16))
    out = shape((own, cells), F32)
    scratch = pltpu.VMEM((2 * rows, LANES), F32)
    return call(part(last_kernel, tiles), "last", (out, out), [VMEM] * 5, [scratch] * 2)(got, scal, direct, obs, q)


def solution(mesh):
    return jax.shard_map(
        per_device,
        mesh=mesh,
        in_specs=(
            P(AXES, None, None),
            P(AXES, None),
            P(AXES, None),
            P(),
            P(),
        ),
        out_specs=(P(AXES, None), P(AXES, None)),
        check_vma=False,
    )
```

```python
import functools

import jax
import jax.numpy as jnp
from jax import lax
from jax.experimental import pallas as pl
from jax.experimental.pallas import tpu as pltpu
from jax.sharding import PartitionSpec as P

AXES = ("mem", "grid")
M = 1024
LANES = 128
ROWS = 16
KEEP = 0.125
REACH = 3
SHIFTS = range(-REACH, REACH + 1)
F32 = jnp.float32
BF16 = jnp.bfloat16
VMEM = pl.BlockSpec(memory_space=pltpu.VMEM)
HBM = pl.BlockSpec(memory_space=pltpu.HBM)


def core_index():
    return lax.rem(lax.axis_index("grid"), 2)


def every(ref, t, first, blocks, tiles):
    return ref[pl.ds(first * tiles + t, blocks, stride=tiles), :]


def lay_kernel(tiles, field_ref, halves_ref):
    own = field_ref.shape[0]
    for h in range(2):
        for t in range(tiles):
            cells = pl.ds((h * tiles + t) * LANES, LANES)
            halves_ref[pl.ds(h * own * tiles + t, own, stride=tiles), :] = field_ref[:, cells]


def start_kernel(tiles, right_ref, sent_ref, direct_ref):
    lay_kernel(tiles, right_ref, direct_ref)
    spread_out(direct_ref[...].astype(BF16), sent_ref)


def spread_out(both, sent_ref):
    devices, rows, _ = sent_ref.shape
    low, high = both[:rows], both[rows:]
    for chip in range(devices // 2):
        sent_ref[2 * chip] = low
        sent_ref[2 * chip + 1] = high


def load_kernel(
    tiles, ens_hbm, nbr_hbm, weight_hbm, obs_hbm, mine_ref, ens_ref, share_ref, acc_ref, obs_ref,
    held, mine, nbr_ref, weight_ref, laid, sems, small,
):
    members, blocks, cells = ens_hbm.shape
    half = cells // 2
    core = core_index()
    chunks = blocks // ROWS

    def copies(g):
        span = pl.ds(pl.multiple_of(g * ROWS, ROWS), ROWS)
        out = []
        for slot in range(2):
            col = pl.multiple_of(lax.rem(core + slot, 2) * half, half)
            source = ens_hbm.at[:, span, pl.ds(col, half)]
            out.append(pltpu.make_async_copy(source, held.at[slot, :, span], sems.at[slot, g]))
        return out

    lists = (
        pltpu.make_async_copy(nbr_hbm, nbr_ref, small.at[0]),
        pltpu.make_async_copy(weight_hbm, weight_ref, small.at[1]),
        pltpu.make_async_copy(obs_hbm, laid, small.at[2]),
    )
    for copy in lists:
        copy.start()

    def begin(g, _):
        for copy in copies(g):
            copy.start()
        return 0

    lax.fori_loop(0, chunks, begin, 0)
    mine[...] = mine_ref[...].astype(F32)
    for copy in lists:
        copy.wait()
    lay_kernel(tiles, laid, obs_ref)
    away = nbr_ref[...] - lax.broadcasted_iota(jnp.int32, nbr_ref.shape, 1)
    away = jnp.where(away > blocks // 2, away - blocks, away)
    away = jnp.where(away < -(blocks // 2), away + blocks, away)
    row = lax.broadcasted_iota(jnp.int32, (8, blocks), 0)
    shares = jnp.zeros((8, blocks), F32)
    for i, shift in enumerate(SHIFTS):
        share = jnp.sum(jnp.where(away == shift, weight_ref[...], 0.0), axis=0, keepdims=True)
        shares = jnp.where(row == i, share, shares)
    shares = shares.T
    for i in range(len(SHIFTS)):
        share_ref[i] = jnp.broadcast_to(shares[:, i : i + 1], (blocks, LANES))

    def group(g, _):
        first = pl.multiple_of(g * ROWS, ROWS)
        for copy in copies(g):
            copy.wait()
        parts = [every(mine, t, first, ROWS, tiles) for t in range(tiles)]
        for k in range(members):
            acc = None
            for t in range(tiles):
                cells = pl.ds(t * LANES, LANES)
                one = held[0, k, pl.ds(first, ROWS), cells].astype(F32)
                ens_ref[0, k, pl.ds(first, ROWS), cells] = one
                acc = one * parts[t] if acc is None else acc + one * parts[t]
            acc_ref[k, pl.ds(first, ROWS), :] = acc
            for t in range(tiles):
                cells = pl.ds(t * LANES, LANES)
                ens_ref[1, k, pl.ds(first, ROWS), cells] = held[1, k, pl.ds(first, ROWS), cells].astype(F32)
        return 0

    lax.fori_loop(0, chunks, group, 0)


def groups(blocks, rows, unroll, body):
    def group(g, _):
        body(g * rows if isinstance(g, int) else pl.multiple_of(g * rows, rows))
        return 0

    lax.fori_loop(0, blocks // rows, group, 0, unroll=unroll)


def own_sums_kernel(tiles, ens_ref, mine_ref, acc_ref, mine):
    _, members, blocks, _ = ens_ref.shape
    mine[...] = mine_ref[...].astype(F32)

    def body(first):
        parts = [every(mine, t, first, 8, tiles) for t in range(tiles)]
        for k in range(members):
            acc = None
            for t in range(tiles):
                term = ens_ref[0, k, pl.ds(first, 8), pl.ds(t * LANES, LANES)] * parts[t]
                acc = term if acc is None else acc + term
            acc_ref[k, pl.ds(first, 8), :] = acc

    groups(blocks, 8, 16, body)


def block_sums(ens_ref, acc_ref, field, sums_ref, tiles):
    _, members, blocks, _ = ens_ref.shape
    lane = lax.broadcasted_iota(jnp.int32, (ROWS, LANES), 1)

    def body(first):
        parts = [every(field, t, first, ROWS, tiles) for t in range(tiles)]
        out = jnp.zeros((ROWS, LANES), F32)
        for k in range(members):
            acc = acc_ref[k, pl.ds(first, ROWS), :]
            for t in range(tiles):
                acc = acc + ens_ref[1, k, pl.ds(first, ROWS), pl.ds(t * LANES, LANES)] * parts[t]
            out = jnp.where(lane == k, jnp.sum(acc, axis=1, keepdims=True), out)
        sums_ref[pl.ds(first, ROWS), :] = out

    groups(blocks, ROWS, 8, body)


def mixed(sums, pad_ref, share_ref):
    blocks = sums.shape[0]
    pad_ref[pl.ds(8, blocks), :] = sums
    pad_ref[pl.ds(0, 8), :] = sums[blocks - 8 :]
    pad_ref[pl.ds(8 + blocks, 8), :] = sums[:8]
    total = sums
    for i, shift in enumerate(SHIFTS):
        total = total + share_ref[i] * pad_ref[pl.ds(8 + shift, blocks), :]
    return total.astype(BF16).astype(F32)


def half_spread(ens_ref, slot, coeff, wide_ref, out_ref, tiles):
    _, members, blocks, _ = ens_ref.shape
    rows, unroll = (8, 16) if coeff is None else (64, 1)

    def body(first):
        here = None if coeff is None else coeff[pl.ds(first, rows), :]
        acc = [None] * tiles
        for k in range(members):
            if here is None:
                one = wide_ref[k, pl.ds(first, rows), :]
            else:
                one = jnp.broadcast_to(here[:, k : k + 1], (rows, LANES))
                wide_ref[k, pl.ds(first, rows), :] = one
            for t in range(tiles):
                term = ens_ref[slot, k, pl.ds(first, rows), pl.ds(t * LANES, LANES)] * one
                acc[t] = term if acc[t] is None else acc[t] + term
        for t in range(tiles):
            out_ref[pl.ds(first * tiles + t, rows, stride=tiles), :] = acc[t]

    groups(blocks, rows, unroll, body)


def first_kernel(tiles, ens_ref, acc_ref, other_ref, share_ref, send_ref, sums_ref, wide_ref, other, pad_ref, coeff_ref):
    other[...] = other_ref[...].astype(F32)
    block_sums(ens_ref, acc_ref, other, sums_ref, tiles)
    coeff_ref[...] = mixed(sums_ref[...], pad_ref, share_ref)
    half_spread(ens_ref, 1, coeff_ref, wide_ref, send_ref, tiles)


def own_kernel(tiles, ens_ref, wide_ref, own_ref):
    half_spread(ens_ref, 0, None, wide_ref, own_ref, tiles)


def received(got, rows):
    devices = got.shape[0]
    sums = []
    for core in range(2):
        total = None
        for chip in range(devices // 2):
            one = got[2 * chip + core, :rows, :].astype(F32)
            total = one if total is None else total + one
        sums.append(total)
    return jnp.concatenate(sums, axis=0)


def middle_kernel(tiles, got_ref, direct_ref, obs_ref, q_ref, sent_ref):
    _, rows, _ = got_ref.shape
    direct = direct_ref[...]
    q = obs_ref[...] * direct + received(got_ref, rows) * (1.0 / M)
    q_ref[...] = q
    d = direct.astype(BF16).astype(F32)
    dd = jnp.sum(direct * d, axis=1, keepdims=True)
    qd = jnp.sum(d * q, axis=1, keepdims=True)
    row = lax.broadcasted_iota(jnp.int32, dd.shape, 0) % rows // tiles
    tau = jnp.zeros_like(dd)
    for b in range(rows // tiles):
        here = row == b
        self = jnp.sum(jnp.where(here, dd, 0.0), axis=0, keepdims=True)
        prod = jnp.sum(jnp.where(here, qd, 0.0), axis=0, keepdims=True)
        share = jnp.where(self > 0.0, (1.0 - KEEP) * prod / jnp.where(self > 0.0, self, 1.0), 0.0)
        tau = jnp.where(here, share, tau)
    spread_out((q - tau * direct).astype(BF16), sent_ref)


def second_kernel(
    tiles, ens_ref, acc_ref, dm_ref, do_ref, pm_ref, po_ref, share_ref, sums0_ref, direct_ref, q_ref, obs_ref,
    send_ref, wide_ref, scal_ref, extra_ref, mine, other, dm, do, sums_ref, pad_ref, coeff_ref,
):
    blocks = ens_ref.shape[2]
    mine[...] = pm_ref[...].astype(F32)
    other[...] = po_ref[...].astype(F32)
    dm[...] = dm_ref[...].astype(F32)
    do[...] = do_ref[...].astype(F32)
    block_sums(ens_ref, acc_ref, other, sums_ref, tiles)
    prod = jnp.zeros((blocks, LANES), F32)
    self = jnp.zeros((blocks, LANES), F32)
    halves = ((dm, mine), (do, other))
    for d_ref, p_ref in halves:
        for t in range(tiles):
            d = every(d_ref, t, 0, blocks, tiles)
            prod = prod + d * every(p_ref, t, 0, blocks, tiles)
            self = self + d * d
    pd = jnp.sum(prod, axis=1, keepdims=True)
    dd = jnp.sum(self, axis=1, keepdims=True)
    tau = jnp.where(dd > 0.0, (1.0 / KEEP - 1.0) * pd / jnp.where(dd > 0.0, dd, 1.0), 0.0)
    rr0 = jnp.sum(dd, axis=0, keepdims=True)
    alpha = rr0 / jnp.sum(pd + tau * dd, axis=0, keepdims=True)
    keep = 1.0 - alpha * tau
    left = jnp.zeros((blocks, LANES), F32)
    for d_ref, p_ref in halves:
        for t in range(tiles):
            r = keep * every(d_ref, t, 0, blocks, tiles) - alpha * every(p_ref, t, 0, blocks, tiles)
            left = left + r * r
    rr1 = jnp.sum(jnp.sum(left, axis=1, keepdims=True), axis=0, keepdims=True)
    beta = rr1 / rr0
    sums = (beta + keep) * sums0_ref[...] - alpha * sums_ref[...]
    coeff = mixed(sums, pad_ref, share_ref)
    coeff_ref[...] = coeff
    direction = (1.0 + beta) * direct_ref[...] - alpha * q_ref[...]
    part = jnp.sum(jnp.sum(sums * coeff, axis=0, keepdims=True), axis=1, keepdims=True) * (1.0 / M)
    part += jnp.sum(jnp.sum(obs_ref[...] * direction * direction, axis=0, keepdims=True), axis=1, keepdims=True)
    row = lax.broadcasted_iota(jnp.int32, (8, LANES), 0)
    scal_ref[...] = jnp.where(row == 0, alpha, jnp.where(row == 1, beta, rr1))
    high = part.astype(BF16).astype(F32)
    mid = (part - high).astype(BF16).astype(F32)
    extra_ref[...] = jnp.where(row == 0, high, jnp.where(row == 1, mid, jnp.where(row == 2, part - high - mid, 0.0)))
    half_spread(ens_ref, 1, coeff_ref, wide_ref, send_ref, tiles)


def last_kernel(tiles, got_ref, scal_ref, direct_ref, obs_ref, q_ref, solution_ref, residual_ref, sol, res):
    devices, rows, _ = got_ref.shape
    rows -= 8
    denom = jnp.zeros((8, LANES), F32)
    for i in range(devices):
        denom = denom + got_ref[i, rows:, :].astype(F32)
    denom = jnp.sum(denom, axis=0, keepdims=True)
    alpha, beta, rr1 = scal_ref[0:1, :], scal_ref[1:2, :], scal_ref[2:3, :]
    direct = direct_ref[...]
    residual = direct - alpha * q_ref[...]
    direction = residual + beta * direct
    image = obs_ref[...] * direction + received(got_ref, rows) * (1.0 / M)
    alpha1 = rr1 / denom
    sol[...] = alpha * direct + alpha1 * direction
    res[...] = residual - alpha1 * image
    own = solution_ref.shape[0]
    for h in range(2):
        for t in range(tiles):
            cells = pl.ds((h * tiles + t) * LANES, LANES)
            at = pl.ds(h * rows + t, own, stride=tiles)
            solution_ref[:, cells] = sol[at, :]
            residual_ref[:, cells] = res[at, :]


def call(kernel, name, outs, ins, scratch=(), mib=8, cost=(0, 0)):
    return pl.pallas_call(
        kernel,
        name=name,
        out_shape=tuple(outs),
        in_specs=ins,
        out_specs=(VMEM,) * len(outs),
        scratch_shapes=list(scratch),
        compiler_params=pltpu.CompilerParams(vmem_limit_bytes=mib * 1024 * 1024),
        cost_estimate=pl.CostEstimate(flops=cost[0], bytes_accessed=cost[1], transcendentals=0),
    )


def per_device(ensemble, right_side, obs_prec, neighbors, loc_weight):
    own, cells = right_side.shape
    members, blocks, _ = ensemble.shape
    devices = lax.axis_size(AXES)
    tiles = cells // (2 * LANES)
    rows = own * tiles
    half = blocks * tiles
    pairs = [(i, i ^ 1) for i in range(devices)]
    shape = jax.ShapeDtypeStruct
    part = functools.partial
    mib = 4 + 4 * blocks // 128

    def swap(x):
        return lax.ppermute(x, AXES, pairs)

    def exchange(x):
        return lax.all_to_all(x, AXES, split_axis=0, concat_axis=0, tiled=True)

    to_all = shape((devices, rows, LANES), BF16)
    lanes = shape((members, blocks, LANES), F32)
    table = shape((blocks, LANES), F32)
    part_half = shape((half, LANES), F32)
    mine = shape((2 * rows, LANES), F32)
    field = pltpu.VMEM((half, LANES), F32)
    padded = pltpu.VMEM((blocks + 16, LANES), F32)
    work = 2 * members * blocks * cells

    sent, direct = call(part(start_kernel, tiles), "start", (to_all, mine), [VMEM])(right_side)
    d_mine = exchange(sent).reshape(half, LANES)
    d_other = swap(d_mine)
    ens, share, acc, obs = call(
        part(load_kernel, tiles),
        "load",
        (shape((2, members, blocks, cells // 2), F32), shape((len(SHIFTS), blocks, LANES), F32), lanes, mine),
        [HBM, HBM, HBM, HBM, VMEM],
        [
            pltpu.VMEM((2, members, blocks, cells // 2), BF16),
            field,
            pltpu.VMEM(neighbors.shape[::-1], jnp.int32),
            pltpu.VMEM(loc_weight.shape[::-1], F32),
            pltpu.VMEM((own, cells), F32),
            pltpu.SemaphoreType.DMA((2, blocks // ROWS)),
            pltpu.SemaphoreType.DMA((3,)),
        ],
        mib=8 + mib,
        cost=(work, 6 * members * blocks * cells),
    )(*(pltpu.with_memory_space_constraint(x, pltpu.HBM) for x in (ensemble, neighbors.T, loc_weight.T, obs_prec)), d_mine)

    coeffs = pltpu.VMEM((blocks, LANES), F32)
    send, sums0, wide = call(
        part(first_kernel, tiles), "first", (part_half, table, lanes), [VMEM] * 4, [field, padded, coeffs],
        mib=mib, cost=(work, 0),
    )(ens, acc, d_other, share)
    (kept,) = call(part(own_kernel, tiles), "own", (part_half,), [VMEM] * 2, mib=mib, cost=(work, 0))(ens, wide)
    got = exchange((kept + swap(send)).astype(BF16).reshape(to_all.shape))

    q, sent = call(part(middle_kernel, tiles), "middle", (mine, to_all), [VMEM] * 3)(got, direct, obs)
    p_mine = exchange(sent).reshape(half, LANES)
    p_other = swap(p_mine)

    small = shape((8, LANES), F32)
    (acc,) = call(part(own_sums_kernel, tiles), "sums", (lanes,), [VMEM] * 2, [field], mib=mib, cost=(work, 0))(ens, p_mine)
    send, wide, scal, extra = call(
        part(second_kernel, tiles),
        "second",
        (part_half, lanes, small, small),
        [VMEM] * 11,
        [field] * 4 + [coeffs, padded, coeffs],
        mib=mib, cost=(work, 0),
    )(ens, acc, d_mine, d_other, p_mine, p_other, share, sums0, direct, q, obs)
    (kept,) = call(part(own_kernel, tiles), "own", (part_half,), [VMEM] * 2, mib=mib, cost=(work, 0))(ens, wide)
    both = (kept + swap(send)).reshape(to_all.shape)
    both = jnp.concatenate([both, jnp.broadcast_to(extra[None], (devices, 8, LANES))], axis=1)
    got = exchange(both.astype(BF16))
    out = shape((own, cells), F32)
    scratch = pltpu.VMEM((2 * rows, LANES), F32)
    return call(part(last_kernel, tiles), "last", (out, out), [VMEM] * 5, [scratch] * 2)(got, scal, direct, obs, q)


def solution(mesh):
    return jax.shard_map(
        per_device,
        mesh=mesh,
        in_specs=(
            P(AXES, None, None),
            P(AXES, None),
            P(AXES, None),
            P(),
            P(),
        ),
        out_specs=(P(AXES, None), P(AXES, None)),
        check_vma=False,
    )
```

```python
import functools

import jax
import jax.numpy as jnp
from jax import lax
from jax.experimental import pallas as pl
from jax.experimental.pallas import tpu as pltpu
from jax.sharding import PartitionSpec as P

AXES = ("mem", "grid")
M = 1024
LANES = 128
ROWS = 16
KEEP = 0.125
REACH = 3
SHIFTS = range(-REACH, REACH + 1)
F32 = jnp.float32
BF16 = jnp.bfloat16
VMEM = pl.BlockSpec(memory_space=pltpu.VMEM)
HBM = pl.BlockSpec(memory_space=pltpu.HBM)


def core_index():
    return lax.rem(lax.axis_index("grid"), 2)


def every(ref, t, first, blocks, tiles):
    return ref[pl.ds(first * tiles + t, blocks, stride=tiles), :]


def lay_kernel(tiles, field_ref, halves_ref):
    own = field_ref.shape[0]
    for h in range(2):
        for t in range(tiles):
            cells = pl.ds((h * tiles + t) * LANES, LANES)
            halves_ref[pl.ds(h * own * tiles + t, own, stride=tiles), :] = field_ref[:, cells]


def start_kernel(tiles, right_ref, sent_ref, direct_ref):
    lay_kernel(tiles, right_ref, direct_ref)
    spread_out(direct_ref[...].astype(BF16), sent_ref)


def spread_out(both, sent_ref):
    devices, rows, _ = sent_ref.shape
    low, high = both[:rows], both[rows:]
    for chip in range(devices // 2):
        sent_ref[2 * chip] = low
        sent_ref[2 * chip + 1] = high


def load_kernel(
    tiles, ens_hbm, nbr_hbm, weight_hbm, obs_hbm, mine_ref, ens_ref, share_ref, acc_ref, obs_ref, mine,
    held, nbr_ref, weight_ref, laid, sems, small,
):
    members, blocks, cells = ens_hbm.shape
    half = cells // 2
    core = core_index()
    each = sems.shape[1]
    chunks, each = each, members // each

    def copies(c):
        span = pl.ds(c * each, each)
        out = []
        for slot in range(2):
            col = pl.multiple_of(lax.rem(core + slot, 2) * half, half)
            source = ens_hbm.at[span, :, pl.ds(col, half)]
            out.append(pltpu.make_async_copy(source, held.at[slot, span], sems.at[slot, c]))
        return out

    lists = (
        pltpu.make_async_copy(nbr_hbm, nbr_ref, small.at[0]),
        pltpu.make_async_copy(weight_hbm, weight_ref, small.at[1]),
        pltpu.make_async_copy(obs_hbm, laid, small.at[2]),
    )
    for copy in lists:
        copy.start()

    def begin(c, _):
        for copy in copies(c):
            copy.start()
        return 0

    lax.fori_loop(0, chunks, begin, 0)
    mine[...] = mine_ref[...].astype(F32)
    for copy in lists:
        copy.wait()
    lay_kernel(tiles, laid, obs_ref)
    away = nbr_ref[...] - lax.broadcasted_iota(jnp.int32, nbr_ref.shape, 1)
    away = jnp.where(away > blocks // 2, away - blocks, away)
    away = jnp.where(away < -(blocks // 2), away + blocks, away)
    row = lax.broadcasted_iota(jnp.int32, (8, blocks), 0)
    shares = jnp.zeros((8, blocks), F32)
    for i, shift in enumerate(SHIFTS):
        share = jnp.sum(jnp.where(away == shift, weight_ref[...], 0.0), axis=0, keepdims=True)
        shares = jnp.where(row == i, share, shares)
    shares = shares.T
    for i in range(len(SHIFTS)):
        share_ref[i] = jnp.broadcast_to(shares[:, i : i + 1], (blocks, LANES))

    def chunk(c, _):
        for copy in copies(c):
            copy.wait()

        def body(first):
            here = pl.ds(first, ROWS)
            parts = [every(mine, t, first, ROWS, tiles) for t in range(tiles)]
            for i in range(each):
                k = c * each + i
                acc = None
                for t in range(tiles):
                    cells = pl.ds(t * LANES, LANES)
                    one = held[0, k, here, cells].astype(F32)
                    ens_ref[0, k, here, cells] = one
                    acc = one * parts[t] if acc is None else acc + one * parts[t]
                acc_ref[k, here, :] = acc
                for t in range(tiles):
                    cells = pl.ds(t * LANES, LANES)
                    ens_ref[1, k, here, cells] = held[1, k, here, cells].astype(F32)

        groups(blocks, ROWS, 8, body)
        return 0

    lax.fori_loop(0, chunks, chunk, 0)


def groups(blocks, rows, unroll, body):
    def group(g, _):
        body(g * rows if isinstance(g, int) else pl.multiple_of(g * rows, rows))
        return 0

    lax.fori_loop(0, blocks // rows, group, 0, unroll=unroll)


def own_sums_kernel(tiles, ens_ref, mine_ref, dm_ref, do_ref, acc_ref, dd_ref, pd_ref, pp_ref, mine):
    _, members, blocks, _ = ens_ref.shape
    mine[...] = mine_ref[...].astype(F32)

    def body(first):
        here = pl.ds(first, 8)
        parts = [every(mine, t, first, 8, tiles) for t in range(tiles)]
        for k in range(members):
            acc_ref[k, here, :] = sum(
                ens_ref[0, k, here, pl.ds(t * LANES, LANES)] * parts[t] for t in range(tiles)
            )
        own = [every(dm_ref, t, first, 8, tiles) for t in range(tiles)]
        far = [every(do_ref, t, first, 8, tiles) for t in range(tiles)]
        dd_ref[here, :] = sum(d * d for d in own + far)
        pd_ref[here, :] = sum(p * d for p, d in zip(parts, own))
        pp_ref[here, :] = sum(p * p for p in parts)

    groups(blocks, 8, 16, body)


def block_sums(ens_ref, acc_ref, field, sums_ref, tiles, also=None):
    _, members, blocks, _ = ens_ref.shape
    lane = lax.broadcasted_iota(jnp.int32, (ROWS, LANES), 1)

    def body(first):
        parts = [every(field, t, first, ROWS, tiles) for t in range(tiles)]
        out = jnp.zeros((ROWS, LANES), F32)
        for k in range(members):
            acc = acc_ref[k, pl.ds(first, ROWS), :]
            for t in range(tiles):
                acc = acc + ens_ref[1, k, pl.ds(first, ROWS), pl.ds(t * LANES, LANES)] * parts[t]
            out = jnp.where(lane == k, jnp.sum(acc, axis=1, keepdims=True), out)
        sums_ref[pl.ds(first, ROWS), :] = out
        if also is not None:
            also(first, parts)

    groups(blocks, ROWS, 8, body)


def mixed(sums, pad_ref, share_ref):
    blocks = sums.shape[0]
    pad_ref[pl.ds(8, blocks), :] = sums
    pad_ref[pl.ds(0, 8), :] = sums[blocks - 8 :]
    pad_ref[pl.ds(8 + blocks, 8), :] = sums[:8]
    total = sums
    for i, shift in enumerate(SHIFTS):
        total = total + share_ref[i] * pad_ref[pl.ds(8 + shift, blocks), :]
    return total.astype(BF16).astype(F32)


def half_spread(ens_ref, slot, coeff, wide_ref, out_ref, tiles):
    _, members, blocks, _ = ens_ref.shape
    rows, unroll = (8, 16) if coeff is None else (16, 8)

    def body(first):
        here = None if coeff is None else coeff[pl.ds(first, rows), :]
        acc = [None] * tiles
        for k in range(members):
            if here is None:
                one = wide_ref[k, pl.ds(first, rows), :]
            else:
                one = jnp.broadcast_to(here[:, k : k + 1].astype(BF16), (rows, LANES)).astype(F32)
                wide_ref[k, pl.ds(first, rows), :] = one
            for t in range(tiles):
                term = ens_ref[slot, k, pl.ds(first, rows), pl.ds(t * LANES, LANES)] * one
                acc[t] = term if acc[t] is None else acc[t] + term
        for t in range(tiles):
            out_ref[pl.ds(first * tiles + t, rows, stride=tiles), :] = acc[t]

    groups(blocks, rows, unroll, body)


def first_kernel(tiles, ens_ref, acc_ref, other_ref, share_ref, send_ref, sums_ref, wide_ref, other, pad_ref, coeff_ref):
    other[...] = other_ref[...].astype(F32)
    block_sums(ens_ref, acc_ref, other, sums_ref, tiles)
    coeff_ref[...] = mixed(sums_ref[...], pad_ref, share_ref)
    half_spread(ens_ref, 1, coeff_ref, wide_ref, send_ref, tiles)


def own_kernel(tiles, ens_ref, wide_ref, own_ref):
    half_spread(ens_ref, 0, None, wide_ref, own_ref, tiles)


def received(got, rows):
    devices = got.shape[0]
    sums = []
    for core in range(2):
        total = None
        for chip in range(devices // 2):
            one = got[2 * chip + core, :rows, :].astype(F32)
            total = one if total is None else total + one
        sums.append(total)
    return jnp.concatenate(sums, axis=0)


def middle_kernel(tiles, got_ref, direct_ref, obs_ref, q_ref, sent_ref):
    _, rows, _ = got_ref.shape
    direct = direct_ref[...]
    q = obs_ref[...] * direct + received(got_ref, rows) * (1.0 / M)
    q_ref[...] = q
    d = direct.astype(BF16).astype(F32)
    dd = jnp.sum(direct * d, axis=1, keepdims=True)
    qd = jnp.sum(d * q, axis=1, keepdims=True)
    row = lax.broadcasted_iota(jnp.int32, dd.shape, 0) % rows // tiles
    tau = jnp.zeros_like(dd)
    for b in range(rows // tiles):
        here = row == b
        self = jnp.sum(jnp.where(here, dd, 0.0), axis=0, keepdims=True)
        prod = jnp.sum(jnp.where(here, qd, 0.0), axis=0, keepdims=True)
        share = jnp.where(self > 0.0, (1.0 - KEEP) * prod / jnp.where(self > 0.0, self, 1.0), 0.0)
        tau = jnp.where(here, share, tau)
    spread_out((q - tau * direct).astype(BF16), sent_ref)


def second_kernel(
    tiles, ens_ref, acc_ref, dd_ref, pd_ref, pp_ref, do_ref, po_ref, share_ref, sums0_ref,
    send_ref, wide_ref, scal_ref, sums_ref, coeff_ref, other, pd_all, pp_all, pad_ref,
):
    blocks = ens_ref.shape[2]
    other[...] = po_ref[...].astype(F32)

    def products(first):
        here = pl.ds(first, ROWS)
        parts = [every(other, t, first, ROWS, tiles) for t in range(tiles)]
        far = [every(do_ref, t, first, ROWS, tiles) for t in range(tiles)]
        pd_all[here, :] = pd_ref[here, :] + sum(p * d for p, d in zip(parts, far))
        pp_all[here, :] = pp_ref[here, :] + sum(p * p for p in parts)

    groups(blocks, ROWS, 8, products)
    dd = jnp.sum(dd_ref[...], axis=1, keepdims=True)
    pd = jnp.sum(pd_all[...], axis=1, keepdims=True)
    pp = jnp.sum(pp_all[...], axis=1, keepdims=True)
    tau = jnp.where(dd > 0.0, (1.0 / KEEP - 1.0) * pd / jnp.where(dd > 0.0, dd, 1.0), 0.0)
    rr0 = jnp.sum(dd, axis=0, keepdims=True)
    alpha = rr0 / jnp.sum(pd + tau * dd, axis=0, keepdims=True)
    keep = 1.0 - alpha * tau
    rr1 = jnp.sum(keep * (keep * dd - 2.0 * alpha * pd) + alpha * alpha * pp, axis=0, keepdims=True)
    beta = rr1 / rr0
    row = lax.broadcasted_iota(jnp.int32, (8, LANES), 0)
    scal_ref[...] = jnp.where(row == 0, alpha, jnp.where(row == 1, beta, rr1))
    block_sums(ens_ref, acc_ref, other, sums_ref, tiles)
    sums = (beta + keep) * sums0_ref[...] - alpha * sums_ref[...]
    sums_ref[...] = sums
    coeff_ref[...] = mixed(sums, pad_ref, share_ref)
    half_spread(ens_ref, 1, coeff_ref, wide_ref, send_ref, tiles)


def second_own_kernel(
    tiles, ens_ref, wide_ref, sums_ref, coeff_ref, scal_ref, direct_ref, q_ref, obs_ref, own_ref, extra_ref
):
    alpha, beta = scal_ref[0:1, :], scal_ref[1:2, :]
    direction = (1.0 + beta) * direct_ref[...] - alpha * q_ref[...]
    part = jnp.sum(jnp.sum(sums_ref[...] * coeff_ref[...], axis=0, keepdims=True), axis=1, keepdims=True) * (1.0 / M)
    part += jnp.sum(jnp.sum(obs_ref[...] * direction * direction, axis=0, keepdims=True), axis=1, keepdims=True)
    row = lax.broadcasted_iota(jnp.int32, (8, LANES), 0)
    high = part.astype(BF16).astype(F32)
    mid = (part - high).astype(BF16).astype(F32)
    extra_ref[...] = jnp.where(row == 0, high, jnp.where(row == 1, mid, jnp.where(row == 2, part - high - mid, 0.0)))
    half_spread(ens_ref, 0, None, wide_ref, own_ref, tiles)


def last_kernel(tiles, got_ref, scal_ref, direct_ref, obs_ref, q_ref, solution_ref, residual_ref, sol, res):
    devices, rows, _ = got_ref.shape
    rows -= 8
    denom = jnp.zeros((8, LANES), F32)
    for i in range(devices):
        denom = denom + got_ref[i, rows:, :].astype(F32)
    denom = jnp.sum(denom, axis=0, keepdims=True)
    alpha, beta, rr1 = scal_ref[0:1, :], scal_ref[1:2, :], scal_ref[2:3, :]
    direct = direct_ref[...]
    residual = direct - alpha * q_ref[...]
    direction = residual + beta * direct
    image = obs_ref[...] * direction + received(got_ref, rows) * (1.0 / M)
    alpha1 = rr1 / denom
    sol[...] = alpha * direct + alpha1 * direction
    res[...] = residual - alpha1 * image
    own = solution_ref.shape[0]
    for h in range(2):
        for t in range(tiles):
            cells = pl.ds((h * tiles + t) * LANES, LANES)
            at = pl.ds(h * rows + t, own, stride=tiles)
            solution_ref[:, cells] = sol[at, :]
            residual_ref[:, cells] = res[at, :]


def call(kernel, name, outs, ins, scratch=(), mib=8, cost=(0, 0)):
    return pl.pallas_call(
        kernel,
        name=name,
        out_shape=tuple(outs),
        in_specs=ins,
        out_specs=(VMEM,) * len(outs),
        scratch_shapes=list(scratch),
        compiler_params=pltpu.CompilerParams(vmem_limit_bytes=mib * 1024 * 1024),
        cost_estimate=pl.CostEstimate(flops=cost[0], bytes_accessed=cost[1], transcendentals=0),
    )


def per_device(ensemble, right_side, obs_prec, neighbors, loc_weight):
    own, cells = right_side.shape
    members, blocks, _ = ensemble.shape
    devices = lax.axis_size(AXES)
    tiles = cells // (2 * LANES)
    rows = own * tiles
    half = blocks * tiles
    pairs = [(i, i ^ 1) for i in range(devices)]
    shape = jax.ShapeDtypeStruct
    part = functools.partial
    mib = 4 + 4 * blocks // 128

    def swap(x):
        return lax.ppermute(x, AXES, pairs)

    def exchange(x):
        return lax.all_to_all(x, AXES, split_axis=0, concat_axis=0, tiled=True)

    to_all = shape((devices, rows, LANES), BF16)
    lanes = shape((members, blocks, LANES), F32)
    table = shape((blocks, LANES), F32)
    part_half = shape((half, LANES), F32)
    mine = shape((2 * rows, LANES), F32)
    field = pltpu.VMEM((half, LANES), F32)
    padded = pltpu.VMEM((blocks + 16, LANES), F32)
    work = 2 * members * blocks * cells

    sent, direct = call(part(start_kernel, tiles), "start", (to_all, mine), [VMEM])(right_side)
    d_mine = exchange(sent).reshape(half, LANES)
    d_other = swap(d_mine)
    ens, share, acc, obs, d_mine = call(
        part(load_kernel, tiles),
        "load",
        (shape((2, members, blocks, cells // 2), F32), shape((len(SHIFTS), blocks, LANES), F32), lanes, mine, part_half),
        [HBM, HBM, HBM, HBM, VMEM],
        [
            pltpu.VMEM((2, members, blocks, cells // 2), BF16),
            pltpu.VMEM(neighbors.shape[::-1], jnp.int32),
            pltpu.VMEM(loc_weight.shape[::-1], F32),
            pltpu.VMEM((own, cells), F32),
            pltpu.SemaphoreType.DMA((2, members // 2)),
            pltpu.SemaphoreType.DMA((3,)),
        ],
        mib=8 + mib,
        cost=(work, 6 * members * blocks * cells),
    )(*(pltpu.with_memory_space_constraint(x, pltpu.HBM) for x in (ensemble, neighbors.T, loc_weight.T, obs_prec)), d_mine)

    coeffs = pltpu.VMEM((blocks, LANES), F32)
    send, sums0, wide, d_other = call(
        part(first_kernel, tiles), "first", (part_half, table, lanes, part_half), [VMEM] * 4, [padded, coeffs],
        mib=mib, cost=(work, 0),
    )(ens, acc, d_other, share)
    (kept,) = call(part(own_kernel, tiles), "own", (part_half,), [VMEM] * 2, mib=mib, cost=(work, 0))(ens, wide)
    got = exchange((kept + swap(send)).astype(BF16).reshape(to_all.shape))

    q, sent = call(part(middle_kernel, tiles), "middle", (mine, to_all), [VMEM] * 3)(got, direct, obs)
    p_mine = exchange(sent).reshape(half, LANES)
    p_other = swap(p_mine)

    small = shape((8, LANES), F32)
    acc, dd, pd, pp = call(
        part(own_sums_kernel, tiles), "sums", (lanes, table, table, table), [VMEM] * 4, [field], mib=mib, cost=(work, 0)
    )(ens, p_mine, d_mine, d_other)
    send, wide, scal, sums, coeff = call(
        part(second_kernel, tiles),
        "second",
        (part_half, lanes, small, table, table),
        [VMEM] * 9,
        [field, coeffs, coeffs, padded],
        mib=mib,
        cost=(work, 0),
    )(ens, acc, dd, pd, pp, d_other, p_other, share, sums0)
    kept, extra = call(
        part(second_own_kernel, tiles), "second_own", (part_half, small), [VMEM] * 8, mib=mib, cost=(work, 0)
    )(ens, wide, sums, coeff, scal, direct, q, obs)
    both = (kept + swap(send)).reshape(to_all.shape)
    both = jnp.concatenate([both, jnp.broadcast_to(extra[None], (devices, 8, LANES))], axis=1)
    got = exchange(both.astype(BF16))
    out = shape((own, cells), F32)
    scratch = pltpu.VMEM((2 * rows, LANES), F32)
    return call(part(last_kernel, tiles), "last", (out, out), [VMEM] * 5, [scratch] * 2)(got, scal, direct, obs, q)


def solution(mesh):
    return jax.shard_map(
        per_device,
        mesh=mesh,
        in_specs=(
            P(AXES, None, None),
            P(AXES, None),
            P(AXES, None),
            P(),
            P(),
        ),
        out_specs=(P(AXES, None), P(AXES, None)),
        check_vma=False,
    )
```

```python
import functools

import jax
import jax.numpy as jnp
from jax import lax
from jax.experimental import pallas as pl
from jax.experimental.pallas import tpu as pltpu
from jax.sharding import PartitionSpec as P

AXES = ("mem", "grid")
M = 1024
LANES = 128
ROWS = 16
KEEP = 0.125
REACH = 3
SHIFTS = range(-REACH, REACH + 1)
F32 = jnp.float32
BF16 = jnp.bfloat16
VMEM = pl.BlockSpec(memory_space=pltpu.VMEM)
HBM = pl.BlockSpec(memory_space=pltpu.HBM)


def core_index():
    return lax.rem(lax.axis_index("grid"), 2)


def every(ref, t, first, blocks, tiles):
    return ref[pl.ds(first * tiles + t, blocks, stride=tiles), :]


def lay_kernel(tiles, field_ref, halves_ref):
    own = field_ref.shape[0]
    for h in range(2):
        for t in range(tiles):
            cells = pl.ds((h * tiles + t) * LANES, LANES)
            halves_ref[pl.ds(h * own * tiles + t, own, stride=tiles), :] = field_ref[:, cells]


def start_kernel(tiles, right_ref, sent_ref, direct_ref):
    lay_kernel(tiles, right_ref, direct_ref)
    spread_out(direct_ref[...].astype(BF16), sent_ref)


def spread_out(both, sent_ref):
    devices, rows, _ = sent_ref.shape
    low, high = both[:rows], both[rows:]
    for chip in range(devices // 2):
        sent_ref[2 * chip] = low
        sent_ref[2 * chip + 1] = high


def load_kernel(
    tiles, ens_hbm, nbr_hbm, weight_hbm, obs_hbm, mine_ref, ens_ref, share_ref, acc_ref, obs_ref, mine,
    held, nbr_ref, weight_ref, laid, sems, small,
):
    members, blocks, cells = ens_hbm.shape
    half = cells // 2
    core = core_index()
    each = sems.shape[1]
    chunks, each = each, members // each

    def copies(c):
        span = pl.ds(c * each, each)
        out = []
        for slot in range(2):
            col = pl.multiple_of(lax.rem(core + slot, 2) * half, half)
            source = ens_hbm.at[span, :, pl.ds(col, half)]
            out.append(pltpu.make_async_copy(source, held.at[slot, span], sems.at[slot, c]))
        return out

    lists = (
        pltpu.make_async_copy(nbr_hbm, nbr_ref, small.at[0]),
        pltpu.make_async_copy(weight_hbm, weight_ref, small.at[1]),
        pltpu.make_async_copy(obs_hbm, laid, small.at[2]),
    )
    for copy in lists:
        copy.start()

    def begin(c, _):
        for copy in copies(c):
            copy.start()
        return 0

    lax.fori_loop(0, chunks, begin, 0)
    mine[...] = mine_ref[...].astype(F32)
    for copy in lists:
        copy.wait()
    lay_kernel(tiles, laid, obs_ref)
    away = nbr_ref[...] - lax.broadcasted_iota(jnp.int32, nbr_ref.shape, 1)
    away = jnp.where(away > blocks // 2, away - blocks, away)
    away = jnp.where(away < -(blocks // 2), away + blocks, away)
    row = lax.broadcasted_iota(jnp.int32, (8, blocks), 0)
    shares = jnp.zeros((8, blocks), F32)
    for i, shift in enumerate(SHIFTS):
        share = jnp.sum(jnp.where(away == shift, weight_ref[...], 0.0), axis=0, keepdims=True)
        shares = jnp.where(row == i, share, shares)
    shares = shares.T
    for i in range(len(SHIFTS)):
        share_ref[i] = jnp.broadcast_to(shares[:, i : i + 1], (blocks, LANES))

    def chunk(c, _):
        for copy in copies(c):
            copy.wait()

        def body(first):
            here = pl.ds(first, ROWS)
            parts = [every(mine, t, first, ROWS, tiles) for t in range(tiles)]
            for i in range(each):
                k = c * each + i
                acc = None
                for t in range(tiles):
                    cells = pl.ds(t * LANES, LANES)
                    one = held[0, k, here, cells].astype(F32)
                    ens_ref[0, k, here, cells] = one
                    acc = one * parts[t] if acc is None else acc + one * parts[t]
                acc_ref[k, here, :] = acc
                for t in range(tiles):
                    cells = pl.ds(t * LANES, LANES)
                    ens_ref[1, k, here, cells] = held[1, k, here, cells].astype(F32)

        groups(blocks, ROWS, 8, body)
        return 0

    lax.fori_loop(0, chunks, chunk, 0)


def groups(blocks, rows, unroll, body):
    def group(g, _):
        body(g * rows if isinstance(g, int) else pl.multiple_of(g * rows, rows))
        return 0

    lax.fori_loop(0, blocks // rows, group, 0, unroll=unroll)


def own_sums_kernel(tiles, ens_ref, mine_ref, dm_ref, do_ref, acc_ref, dd_ref, pd_ref, pp_ref, mine):
    _, members, blocks, _ = ens_ref.shape
    mine[...] = mine_ref[...].astype(F32)

    def body(first):
        here = pl.ds(first, 8)
        parts = [every(mine, t, first, 8, tiles) for t in range(tiles)]
        for k in range(members):
            acc_ref[k, here, :] = sum(
                ens_ref[0, k, here, pl.ds(t * LANES, LANES)] * parts[t] for t in range(tiles)
            )
        own = [every(dm_ref, t, first, 8, tiles) for t in range(tiles)]
        far = [every(do_ref, t, first, 8, tiles) for t in range(tiles)]
        dd_ref[here, :] = sum(d * d for d in own + far)
        pd_ref[here, :] = sum(p * d for p, d in zip(parts, own))
        pp_ref[here, :] = sum(p * p for p in parts)

    groups(blocks, 8, 16, body)


def block_sums(ens_ref, acc_ref, field, sums_ref, tiles, also=None):
    _, members, blocks, _ = ens_ref.shape
    lane = lax.broadcasted_iota(jnp.int32, (ROWS, LANES), 1)

    def body(first):
        parts = [every(field, t, first, ROWS, tiles) for t in range(tiles)]
        out = jnp.zeros((ROWS, LANES), F32)
        for k in range(members):
            acc = acc_ref[k, pl.ds(first, ROWS), :]
            for t in range(tiles):
                acc = acc + ens_ref[1, k, pl.ds(first, ROWS), pl.ds(t * LANES, LANES)] * parts[t]
            out = jnp.where(lane == k, jnp.sum(acc, axis=1, keepdims=True), out)
        sums_ref[pl.ds(first, ROWS), :] = out
        if also is not None:
            also(first, parts)

    groups(blocks, ROWS, 8, body)


def mixed(sums, pad_ref, share_ref):
    blocks = sums.shape[0]
    pad_ref[pl.ds(8, blocks), :] = sums
    pad_ref[pl.ds(0, 8), :] = sums[blocks - 8 :]
    pad_ref[pl.ds(8 + blocks, 8), :] = sums[:8]
    total = sums
    for i, shift in enumerate(SHIFTS):
        total = total + share_ref[i] * pad_ref[pl.ds(8 + shift, blocks), :]
    return total.astype(BF16).astype(F32)


def half_spread(ens_ref, slot, coeff, wide_ref, out_ref, tiles):
    _, members, blocks, _ = ens_ref.shape
    rows, unroll = (8, 16) if coeff is None else (16, 8)

    def body(first):
        here = None if coeff is None else coeff[pl.ds(first, rows), :]
        acc = [None] * tiles
        for k in range(members):
            if here is None:
                one = wide_ref[k, pl.ds(first, rows), :]
            else:
                one = jnp.broadcast_to(here[:, k : k + 1].astype(BF16), (rows, LANES)).astype(F32)
                wide_ref[k, pl.ds(first, rows), :] = one
            for t in range(tiles):
                term = ens_ref[slot, k, pl.ds(first, rows), pl.ds(t * LANES, LANES)] * one
                acc[t] = term if acc[t] is None else acc[t] + term
        for t in range(tiles):
            out_ref[pl.ds(first * tiles + t, rows, stride=tiles), :] = acc[t]

    groups(blocks, rows, unroll, body)


def first_kernel(tiles, ens_ref, acc_ref, other_ref, share_ref, send_ref, sums_ref, wide_ref, other, pad_ref, coeff_ref, spread):
    other[...] = other_ref[...].astype(F32)
    block_sums(ens_ref, acc_ref, other, sums_ref, tiles)
    coeff_ref[...] = mixed(sums_ref[...], pad_ref, share_ref)
    half_spread(ens_ref, 1, coeff_ref, wide_ref, spread, tiles)
    send_ref[...] = spread[...].astype(BF16)


def own_kernel(tiles, ens_ref, wide_ref, own_ref):
    half_spread(ens_ref, 0, None, wide_ref, own_ref, tiles)


def received(got, rows):
    devices = got.shape[0]
    sums = []
    for core in range(2):
        total = None
        for chip in range(devices // 2):
            one = got[2 * chip + core, :rows, :].astype(F32)
            total = one if total is None else total + one
        sums.append(total)
    return jnp.concatenate(sums, axis=0)


def middle_kernel(tiles, got_ref, direct_ref, obs_ref, q_ref, sent_ref):
    _, rows, _ = got_ref.shape
    direct = direct_ref[...]
    q = obs_ref[...] * direct + received(got_ref, rows) * (1.0 / M)
    q_ref[...] = q
    d = direct.astype(BF16).astype(F32)
    dd = jnp.sum(direct * d, axis=1, keepdims=True)
    qd = jnp.sum(d * q, axis=1, keepdims=True)
    row = lax.broadcasted_iota(jnp.int32, dd.shape, 0) % rows // tiles
    tau = jnp.zeros_like(dd)
    for b in range(rows // tiles):
        here = row == b
        self = jnp.sum(jnp.where(here, dd, 0.0), axis=0, keepdims=True)
        prod = jnp.sum(jnp.where(here, qd, 0.0), axis=0, keepdims=True)
        share = jnp.where(self > 0.0, (1.0 - KEEP) * prod / jnp.where(self > 0.0, self, 1.0), 0.0)
        tau = jnp.where(here, share, tau)
    spread_out((q - tau * direct).astype(BF16), sent_ref)


def second_kernel(
    tiles, ens_ref, acc_ref, dd_ref, pd_ref, pp_ref, do_ref, po_ref, share_ref, sums0_ref,
    send_ref, wide_ref, scal_ref, sums_ref, coeff_ref, other, pd_all, pp_all, pad_ref, spread,
):
    blocks = ens_ref.shape[2]
    other[...] = po_ref[...].astype(F32)

    def products(first):
        here = pl.ds(first, ROWS)
        parts = [every(other, t, first, ROWS, tiles) for t in range(tiles)]
        far = [every(do_ref, t, first, ROWS, tiles) for t in range(tiles)]
        pd_all[here, :] = pd_ref[here, :] + sum(p * d for p, d in zip(parts, far))
        pp_all[here, :] = pp_ref[here, :] + sum(p * p for p in parts)

    groups(blocks, ROWS, 8, products)
    dd = jnp.sum(dd_ref[...], axis=1, keepdims=True)
    pd = jnp.sum(pd_all[...], axis=1, keepdims=True)
    pp = jnp.sum(pp_all[...], axis=1, keepdims=True)
    tau = jnp.where(dd > 0.0, (1.0 / KEEP - 1.0) * pd / jnp.where(dd > 0.0, dd, 1.0), 0.0)
    rr0 = jnp.sum(dd, axis=0, keepdims=True)
    alpha = rr0 / jnp.sum(pd + tau * dd, axis=0, keepdims=True)
    keep = 1.0 - alpha * tau
    rr1 = jnp.sum(keep * (keep * dd - 2.0 * alpha * pd) + alpha * alpha * pp, axis=0, keepdims=True)
    beta = rr1 / rr0
    row = lax.broadcasted_iota(jnp.int32, (8, LANES), 0)
    scal_ref[...] = jnp.where(row == 0, alpha, jnp.where(row == 1, beta, rr1))
    block_sums(ens_ref, acc_ref, other, sums_ref, tiles)
    sums = (beta + keep) * sums0_ref[...] - alpha * sums_ref[...]
    sums_ref[...] = sums
    coeff_ref[...] = mixed(sums, pad_ref, share_ref)
    half_spread(ens_ref, 1, coeff_ref, wide_ref, spread, tiles)
    send_ref[...] = spread[...].astype(BF16)


def second_own_kernel(
    tiles, ens_ref, wide_ref, sums_ref, coeff_ref, scal_ref, direct_ref, q_ref, obs_ref, own_ref, extra_ref
):
    alpha, beta = scal_ref[0:1, :], scal_ref[1:2, :]
    direction = (1.0 + beta) * direct_ref[...] - alpha * q_ref[...]
    part = jnp.sum(jnp.sum(sums_ref[...] * coeff_ref[...], axis=0, keepdims=True), axis=1, keepdims=True) * (1.0 / M)
    part += jnp.sum(jnp.sum(obs_ref[...] * direction * direction, axis=0, keepdims=True), axis=1, keepdims=True)
    row = lax.broadcasted_iota(jnp.int32, (8, LANES), 0)
    high = part.astype(BF16).astype(F32)
    mid = (part - high).astype(BF16).astype(F32)
    extra_ref[...] = jnp.where(row == 0, high, jnp.where(row == 1, mid, jnp.where(row == 2, part - high - mid, 0.0)))
    half_spread(ens_ref, 0, None, wide_ref, own_ref, tiles)


def last_kernel(tiles, got_ref, scal_ref, direct_ref, obs_ref, q_ref, solution_ref, residual_ref, sol, res):
    devices, rows, _ = got_ref.shape
    rows -= 8
    denom = jnp.zeros((8, LANES), F32)
    for i in range(devices):
        denom = denom + got_ref[i, rows:, :].astype(F32)
    denom = jnp.sum(denom, axis=0, keepdims=True)
    alpha, beta, rr1 = scal_ref[0:1, :], scal_ref[1:2, :], scal_ref[2:3, :]
    direct = direct_ref[...]
    residual = direct - alpha * q_ref[...]
    direction = residual + beta * direct
    image = obs_ref[...] * direction + received(got_ref, rows) * (1.0 / M)
    alpha1 = rr1 / denom
    sol[...] = alpha * direct + alpha1 * direction
    res[...] = residual - alpha1 * image
    own = solution_ref.shape[0]
    for h in range(2):
        for t in range(tiles):
            cells = pl.ds((h * tiles + t) * LANES, LANES)
            at = pl.ds(h * rows + t, own, stride=tiles)
            solution_ref[:, cells] = sol[at, :]
            residual_ref[:, cells] = res[at, :]


def call(kernel, name, outs, ins, scratch=(), mib=8, cost=(0, 0)):
    return pl.pallas_call(
        kernel,
        name=name,
        out_shape=tuple(outs),
        in_specs=ins,
        out_specs=(VMEM,) * len(outs),
        scratch_shapes=list(scratch),
        compiler_params=pltpu.CompilerParams(vmem_limit_bytes=mib * 1024 * 1024),
        cost_estimate=pl.CostEstimate(flops=cost[0], bytes_accessed=cost[1], transcendentals=0),
    )


def per_device(ensemble, right_side, obs_prec, neighbors, loc_weight):
    own, cells = right_side.shape
    members, blocks, _ = ensemble.shape
    devices = lax.axis_size(AXES)
    tiles = cells // (2 * LANES)
    rows = own * tiles
    half = blocks * tiles
    pairs = [(i, i ^ 1) for i in range(devices)]
    shape = jax.ShapeDtypeStruct
    part = functools.partial
    mib = 4 + 4 * blocks // 128

    def swap(x):
        return lax.ppermute(x, AXES, pairs)

    def exchange(x):
        return lax.all_to_all(x, AXES, split_axis=0, concat_axis=0, tiled=True)

    to_all = shape((devices, rows, LANES), BF16)
    lanes = shape((members, blocks, LANES), F32)
    table = shape((blocks, LANES), F32)
    to_swap = shape((half, LANES), BF16)
    part_half = shape((half, LANES), F32)
    mine = shape((2 * rows, LANES), F32)
    field = pltpu.VMEM((half, LANES), F32)
    padded = pltpu.VMEM((blocks + 16, LANES), F32)
    work = 2 * members * blocks * cells

    sent, direct = call(part(start_kernel, tiles), "start", (to_all, mine), [VMEM])(right_side)
    d_mine = exchange(sent).reshape(half, LANES)
    d_other = swap(d_mine)
    ens, share, acc, obs, d_mine = call(
        part(load_kernel, tiles),
        "load",
        (shape((2, members, blocks, cells // 2), F32), shape((len(SHIFTS), blocks, LANES), F32), lanes, mine, part_half),
        [HBM, HBM, HBM, HBM, VMEM],
        [
            pltpu.VMEM((2, members, blocks, cells // 2), BF16),
            pltpu.VMEM(neighbors.shape[::-1], jnp.int32),
            pltpu.VMEM(loc_weight.shape[::-1], F32),
            pltpu.VMEM((own, cells), F32),
            pltpu.SemaphoreType.DMA((2, members // 2)),
            pltpu.SemaphoreType.DMA((3,)),
        ],
        mib=8 + mib,
        cost=(work, 6 * members * blocks * cells),
    )(*(pltpu.with_memory_space_constraint(x, pltpu.HBM) for x in (ensemble, neighbors.T, loc_weight.T, obs_prec)), d_mine)

    coeffs = pltpu.VMEM((blocks, LANES), F32)
    send, sums0, wide, d_other = call(
        part(first_kernel, tiles), "first", (to_swap, table, lanes, part_half), [VMEM] * 4, [padded, coeffs, field],
        mib=mib, cost=(work, 0),
    )(ens, acc, d_other, share)
    (kept,) = call(part(own_kernel, tiles), "own", (part_half,), [VMEM] * 2, mib=mib, cost=(work, 0))(ens, wide)
    got = exchange((kept + swap(send).astype(F32)).astype(BF16).reshape(to_all.shape))

    q, sent = call(part(middle_kernel, tiles), "middle", (mine, to_all), [VMEM] * 3)(got, direct, obs)
    p_mine = exchange(sent).reshape(half, LANES)
    p_other = swap(p_mine)

    small = shape((8, LANES), F32)
    acc, dd, pd, pp = call(
        part(own_sums_kernel, tiles), "sums", (lanes, table, table, table), [VMEM] * 4, [field], mib=mib, cost=(work, 0)
    )(ens, p_mine, d_mine, d_other)
    send, wide, scal, sums, coeff = call(
        part(second_kernel, tiles),
        "second",
        (to_swap, lanes, small, table, table),
        [VMEM] * 9,
        [field, coeffs, coeffs, padded, field],
        mib=mib,
        cost=(work, 0),
    )(ens, acc, dd, pd, pp, d_other, p_other, share, sums0)
    kept, extra = call(
        part(second_own_kernel, tiles), "second_own", (part_half, small), [VMEM] * 8, mib=mib, cost=(work, 0)
    )(ens, wide, sums, coeff, scal, direct, q, obs)
    both = (kept + swap(send).astype(F32)).reshape(to_all.shape)
    both = jnp.concatenate([both, jnp.broadcast_to(extra[None], (devices, 8, LANES))], axis=1)
    got = exchange(both.astype(BF16))
    out = shape((own, cells), F32)
    scratch = pltpu.VMEM((2 * rows, LANES), F32)
    return call(part(last_kernel, tiles), "last", (out, out), [VMEM] * 5, [scratch] * 2)(got, scal, direct, obs, q)


def solution(mesh):
    return jax.shard_map(
        per_device,
        mesh=mesh,
        in_specs=(
            P(AXES, None, None),
            P(AXES, None),
            P(AXES, None),
            P(),
            P(),
        ),
        out_specs=(P(AXES, None), P(AXES, None)),
        check_vma=False,
    )
```

```python
import functools

import jax
import jax.numpy as jnp
from jax import lax
from jax.experimental import pallas as pl
from jax.experimental.pallas import tpu as pltpu
from jax.sharding import PartitionSpec as P

AXES = ("mem", "grid")
M = 1024
LANES = 128
ROWS = 16
KEEP = 0.125
REACH = 3
SHIFTS = range(-REACH, REACH + 1)
F32 = jnp.float32
BF16 = jnp.bfloat16
VMEM = pl.BlockSpec(memory_space=pltpu.VMEM)
HBM = pl.BlockSpec(memory_space=pltpu.HBM)


def core_index():
    return lax.rem(lax.axis_index("grid"), 2)


def every(ref, t, first, blocks, tiles):
    return ref[pl.ds(first * tiles + t, blocks, stride=tiles), :]


def lay_kernel(tiles, field_ref, halves_ref):
    own = field_ref.shape[0]
    for h in range(2):
        for t in range(tiles):
            cells = pl.ds((h * tiles + t) * LANES, LANES)
            halves_ref[pl.ds(h * own * tiles + t, own, stride=tiles), :] = field_ref[:, cells]


def start_kernel(tiles, right_ref, sent_ref, direct_ref):
    lay_kernel(tiles, right_ref, direct_ref)
    spread_out(direct_ref[...].astype(BF16), sent_ref)


def spread_out(both, sent_ref):
    devices, rows, _ = sent_ref.shape
    low, high = both[:rows], both[rows:]
    for chip in range(devices // 2):
        sent_ref[2 * chip] = low
        sent_ref[2 * chip + 1] = high


def load_kernel(
    tiles, ens_hbm, nbr_hbm, weight_hbm, obs_hbm, mine_ref, ens_ref, share_ref, acc_ref, obs_ref, mine,
    held, nbr_ref, weight_ref, laid, sems, small,
):
    members, blocks, cells = ens_hbm.shape
    half = cells // 2
    core = core_index()
    each = sems.shape[1]
    chunks, each = each, members // each

    def copies(c):
        span = pl.ds(c * each, each)
        out = []
        for slot in range(2):
            col = pl.multiple_of(lax.rem(core + slot, 2) * half, half)
            source = ens_hbm.at[span, :, pl.ds(col, half)]
            out.append(pltpu.make_async_copy(source, held.at[slot, span], sems.at[slot, c]))
        return out

    lists = (
        pltpu.make_async_copy(nbr_hbm, nbr_ref, small.at[0]),
        pltpu.make_async_copy(weight_hbm, weight_ref, small.at[1]),
        pltpu.make_async_copy(obs_hbm, laid, small.at[2]),
    )
    for copy in lists:
        copy.start()

    def begin(c, _):
        for copy in copies(c):
            copy.start()
        return 0

    lax.fori_loop(0, chunks, begin, 0)
    mine[...] = mine_ref[...].astype(F32)
    for copy in lists:
        copy.wait()
    lay_kernel(tiles, laid, obs_ref)
    away = nbr_ref[...] - lax.broadcasted_iota(jnp.int32, nbr_ref.shape, 1)
    away = jnp.where(away > blocks // 2, away - blocks, away)
    away = jnp.where(away < -(blocks // 2), away + blocks, away)
    row = lax.broadcasted_iota(jnp.int32, (8, blocks), 0)
    shares = jnp.zeros((8, blocks), F32)
    for i, shift in enumerate(SHIFTS):
        share = jnp.sum(jnp.where(away == shift, weight_ref[...], 0.0), axis=0, keepdims=True)
        shares = jnp.where(row == i, share, shares)
    shares = shares.T
    for i in range(len(SHIFTS)):
        share_ref[i] = jnp.broadcast_to(shares[:, i : i + 1], (blocks, LANES))

    acc_ref[...] = jnp.zeros_like(acc_ref)
    lane = lax.broadcasted_iota(jnp.int32, (ROWS, LANES), 1)

    def chunk(c, _):
        for copy in copies(c):
            copy.wait()

        def body(first):
            here = pl.ds(first, ROWS)
            parts = [every(mine, t, first, ROWS, tiles) for t in range(tiles)]
            sums = acc_ref[here, :]
            for i in range(each):
                k = c * each + i
                acc = None
                for t in range(tiles):
                    cells = pl.ds(t * LANES, LANES)
                    one = held[0, k, here, cells].astype(F32)
                    ens_ref[0, k, here, cells] = one
                    acc = one * parts[t] if acc is None else acc + one * parts[t]
                sums = jnp.where(lane == k, jnp.sum(acc, axis=1, keepdims=True), sums)
                for t in range(tiles):
                    cells = pl.ds(t * LANES, LANES)
                    ens_ref[1, k, here, cells] = held[1, k, here, cells].astype(F32)
            acc_ref[here, :] = sums

        groups(blocks, ROWS, 8, body)
        return 0

    lax.fori_loop(0, chunks, chunk, 0)


def groups(blocks, rows, unroll, body):
    def group(g, _):
        body(g * rows if isinstance(g, int) else pl.multiple_of(g * rows, rows))
        return 0

    lax.fori_loop(0, blocks // rows, group, 0, unroll=unroll)


def own_sums_kernel(tiles, ens_ref, mine_ref, dm_ref, do_ref, acc_ref, dd_ref, pd_ref, pp_ref, mine):
    blocks = ens_ref.shape[2]
    mine[...] = mine_ref[...].astype(F32)

    half_sums(ens_ref, 0, mine, acc_ref, tiles)

    def body(first):
        here = pl.ds(first, 8)
        parts = [every(mine, t, first, 8, tiles) for t in range(tiles)]
        own = [every(dm_ref, t, first, 8, tiles) for t in range(tiles)]
        far = [every(do_ref, t, first, 8, tiles) for t in range(tiles)]
        dd_ref[here, :] = sum(d * d for d in own + far)
        pd_ref[here, :] = sum(p * d for p, d in zip(parts, own))
        pp_ref[here, :] = sum(p * p for p in parts)

    groups(blocks, 8, 16, body)


def half_sums(ens_ref, slot, field, sums_ref, tiles, start=None):
    _, members, blocks, _ = ens_ref.shape
    lane = lax.broadcasted_iota(jnp.int32, (ROWS, LANES), 1)

    def body(first):
        here = pl.ds(first, ROWS)
        parts = [every(field, t, first, ROWS, tiles) for t in range(tiles)]
        out = jnp.zeros((ROWS, LANES), F32)
        for k in range(members):
            acc = None
            for t in range(tiles):
                term = ens_ref[slot, k, here, pl.ds(t * LANES, LANES)] * parts[t]
                acc = term if acc is None else acc + term
            out = jnp.where(lane == k, jnp.sum(acc, axis=1, keepdims=True), out)
        sums_ref[here, :] = out if start is None else out + start[here, :]

    groups(blocks, ROWS, 8, body)


def mixed(sums, pad_ref, share_ref):
    blocks = sums.shape[0]
    pad_ref[pl.ds(8, blocks), :] = sums
    pad_ref[pl.ds(0, 8), :] = sums[blocks - 8 :]
    pad_ref[pl.ds(8 + blocks, 8), :] = sums[:8]
    total = sums
    for i, shift in enumerate(SHIFTS):
        total = total + share_ref[i] * pad_ref[pl.ds(8 + shift, blocks), :]
    return total.astype(BF16).astype(F32)


def half_spread(ens_ref, slot, coeff, wide_ref, out_ref, tiles):
    _, members, blocks, _ = ens_ref.shape
    rows, unroll = (8, 16) if coeff is None else (16, 8)

    def body(first):
        here = None if coeff is None else coeff[pl.ds(first, rows), :]
        acc = [None] * tiles
        for k in range(members):
            if here is None:
                one = wide_ref[k, pl.ds(first, rows), :]
            else:
                one = jnp.broadcast_to(here[:, k : k + 1].astype(BF16), (rows, LANES)).astype(F32)
                wide_ref[k, pl.ds(first, rows), :] = one
            for t in range(tiles):
                term = ens_ref[slot, k, pl.ds(first, rows), pl.ds(t * LANES, LANES)] * one
                acc[t] = term if acc[t] is None else acc[t] + term
        for t in range(tiles):
            out_ref[pl.ds(first * tiles + t, rows, stride=tiles), :] = acc[t]

    groups(blocks, rows, unroll, body)


def first_kernel(tiles, ens_ref, acc_ref, other_ref, share_ref, send_ref, sums_ref, wide_ref, other, pad_ref, coeff_ref, spread):
    other[...] = other_ref[...].astype(F32)
    half_sums(ens_ref, 1, other, sums_ref, tiles, acc_ref)
    coeff_ref[...] = mixed(sums_ref[...], pad_ref, share_ref)
    half_spread(ens_ref, 1, coeff_ref, wide_ref, spread, tiles)
    send_ref[...] = spread[...].astype(BF16)


def own_kernel(tiles, ens_ref, wide_ref, own_ref):
    half_spread(ens_ref, 0, None, wide_ref, own_ref, tiles)


def received(got, rows):
    devices = got.shape[0]
    sums = []
    for core in range(2):
        total = None
        for chip in range(devices // 2):
            one = got[2 * chip + core, :rows, :].astype(F32)
            total = one if total is None else total + one
        sums.append(total)
    return jnp.concatenate(sums, axis=0)


def middle_kernel(tiles, got_ref, direct_ref, obs_ref, q_ref, sent_ref):
    _, rows, _ = got_ref.shape
    direct = direct_ref[...]
    q = obs_ref[...] * direct + received(got_ref, rows) * (1.0 / M)
    q_ref[...] = q
    d = direct.astype(BF16).astype(F32)
    dd = jnp.sum(direct * d, axis=1, keepdims=True)
    qd = jnp.sum(d * q, axis=1, keepdims=True)
    row = lax.broadcasted_iota(jnp.int32, dd.shape, 0) % rows // tiles
    tau = jnp.zeros_like(dd)
    for b in range(rows // tiles):
        here = row == b
        self = jnp.sum(jnp.where(here, dd, 0.0), axis=0, keepdims=True)
        prod = jnp.sum(jnp.where(here, qd, 0.0), axis=0, keepdims=True)
        share = jnp.where(self > 0.0, (1.0 - KEEP) * prod / jnp.where(self > 0.0, self, 1.0), 0.0)
        tau = jnp.where(here, share, tau)
    spread_out((q - tau * direct).astype(BF16), sent_ref)


def second_kernel(
    tiles, ens_ref, acc_ref, dd_ref, pd_ref, pp_ref, do_ref, po_ref, share_ref, sums0_ref,
    send_ref, wide_ref, scal_ref, sums_ref, coeff_ref, other, pd_all, pp_all, pad_ref, spread,
):
    blocks = ens_ref.shape[2]
    other[...] = po_ref[...].astype(F32)

    def products(first):
        here = pl.ds(first, ROWS)
        parts = [every(other, t, first, ROWS, tiles) for t in range(tiles)]
        far = [every(do_ref, t, first, ROWS, tiles) for t in range(tiles)]
        pd_all[here, :] = pd_ref[here, :] + sum(p * d for p, d in zip(parts, far))
        pp_all[here, :] = pp_ref[here, :] + sum(p * p for p in parts)

    groups(blocks, ROWS, 8, products)
    dd = jnp.sum(dd_ref[...], axis=1, keepdims=True)
    pd = jnp.sum(pd_all[...], axis=1, keepdims=True)
    pp = jnp.sum(pp_all[...], axis=1, keepdims=True)
    tau = jnp.where(dd > 0.0, (1.0 / KEEP - 1.0) * pd / jnp.where(dd > 0.0, dd, 1.0), 0.0)
    rr0 = jnp.sum(dd, axis=0, keepdims=True)
    alpha = rr0 / jnp.sum(pd + tau * dd, axis=0, keepdims=True)
    keep = 1.0 - alpha * tau
    rr1 = jnp.sum(keep * (keep * dd - 2.0 * alpha * pd) + alpha * alpha * pp, axis=0, keepdims=True)
    beta = rr1 / rr0
    row = lax.broadcasted_iota(jnp.int32, (8, LANES), 0)
    scal_ref[...] = jnp.where(row == 0, alpha, jnp.where(row == 1, beta, rr1))
    half_sums(ens_ref, 1, other, sums_ref, tiles, acc_ref)
    sums = (beta + keep) * sums0_ref[...] - alpha * sums_ref[...]
    sums_ref[...] = sums
    coeff_ref[...] = mixed(sums, pad_ref, share_ref)
    half_spread(ens_ref, 1, coeff_ref, wide_ref, spread, tiles)
    send_ref[...] = spread[...].astype(BF16)


def second_own_kernel(
    tiles, ens_ref, wide_ref, sums_ref, coeff_ref, scal_ref, direct_ref, q_ref, obs_ref, own_ref, extra_ref
):
    alpha, beta = scal_ref[0:1, :], scal_ref[1:2, :]
    direction = (1.0 + beta) * direct_ref[...] - alpha * q_ref[...]
    part = jnp.sum(jnp.sum(sums_ref[...] * coeff_ref[...], axis=0, keepdims=True), axis=1, keepdims=True) * (1.0 / M)
    part += jnp.sum(jnp.sum(obs_ref[...] * direction * direction, axis=0, keepdims=True), axis=1, keepdims=True)
    row = lax.broadcasted_iota(jnp.int32, (8, LANES), 0)
    high = part.astype(BF16).astype(F32)
    mid = (part - high).astype(BF16).astype(F32)
    extra_ref[...] = jnp.where(row == 0, high, jnp.where(row == 1, mid, jnp.where(row == 2, part - high - mid, 0.0)))
    half_spread(ens_ref, 0, None, wide_ref, own_ref, tiles)


def last_kernel(tiles, got_ref, scal_ref, direct_ref, obs_ref, q_ref, solution_ref, residual_ref, sol, res):
    devices, rows, _ = got_ref.shape
    rows -= 8
    denom = jnp.zeros((8, LANES), F32)
    for i in range(devices):
        denom = denom + got_ref[i, rows:, :].astype(F32)
    denom = jnp.sum(denom, axis=0, keepdims=True)
    alpha, beta, rr1 = scal_ref[0:1, :], scal_ref[1:2, :], scal_ref[2:3, :]
    direct = direct_ref[...]
    residual = direct - alpha * q_ref[...]
    direction = residual + beta * direct
    image = obs_ref[...] * direction + received(got_ref, rows) * (1.0 / M)
    alpha1 = rr1 / denom
    sol[...] = alpha * direct + alpha1 * direction
    res[...] = residual - alpha1 * image
    own = solution_ref.shape[0]
    for h in range(2):
        for t in range(tiles):
            cells = pl.ds((h * tiles + t) * LANES, LANES)
            at = pl.ds(h * rows + t, own, stride=tiles)
            solution_ref[:, cells] = sol[at, :]
            residual_ref[:, cells] = res[at, :]


def call(kernel, name, outs, ins, scratch=(), mib=8, cost=(0, 0)):
    return pl.pallas_call(
        kernel,
        name=name,
        out_shape=tuple(outs),
        in_specs=ins,
        out_specs=(VMEM,) * len(outs),
        scratch_shapes=list(scratch),
        compiler_params=pltpu.CompilerParams(vmem_limit_bytes=mib * 1024 * 1024),
        cost_estimate=pl.CostEstimate(flops=cost[0], bytes_accessed=cost[1], transcendentals=0),
    )


def per_device(ensemble, right_side, obs_prec, neighbors, loc_weight):
    own, cells = right_side.shape
    members, blocks, _ = ensemble.shape
    devices = lax.axis_size(AXES)
    tiles = cells // (2 * LANES)
    rows = own * tiles
    half = blocks * tiles
    pairs = [(i, i ^ 1) for i in range(devices)]
    shape = jax.ShapeDtypeStruct
    part = functools.partial
    mib = 4 + 4 * blocks // 128

    def swap(x):
        return lax.ppermute(x, AXES, pairs)

    def exchange(x):
        return lax.all_to_all(x, AXES, split_axis=0, concat_axis=0, tiled=True)

    to_all = shape((devices, rows, LANES), BF16)
    lanes = shape((members, blocks, LANES), F32)
    table = shape((blocks, LANES), F32)
    to_swap = shape((half, LANES), BF16)
    part_half = shape((half, LANES), F32)
    mine = shape((2 * rows, LANES), F32)
    field = pltpu.VMEM((half, LANES), F32)
    padded = pltpu.VMEM((blocks + 16, LANES), F32)
    work = 2 * members * blocks * cells

    sent, direct = call(part(start_kernel, tiles), "start", (to_all, mine), [VMEM])(right_side)
    d_mine = exchange(sent).reshape(half, LANES)
    d_other = swap(d_mine)
    ens, share, acc, obs, d_mine = call(
        part(load_kernel, tiles),
        "load",
        (shape((2, members, blocks, cells // 2), F32), shape((len(SHIFTS), blocks, LANES), F32), table, mine, part_half),
        [HBM, HBM, HBM, HBM, VMEM],
        [
            pltpu.VMEM((2, members, blocks, cells // 2), BF16),
            pltpu.VMEM(neighbors.shape[::-1], jnp.int32),
            pltpu.VMEM(loc_weight.shape[::-1], F32),
            pltpu.VMEM((own, cells), F32),
            pltpu.SemaphoreType.DMA((2, members // 4)),
            pltpu.SemaphoreType.DMA((3,)),
        ],
        mib=8 + mib,
        cost=(work, 6 * members * blocks * cells),
    )(*(pltpu.with_memory_space_constraint(x, pltpu.HBM) for x in (ensemble, neighbors.T, loc_weight.T, obs_prec)), d_mine)

    coeffs = pltpu.VMEM((blocks, LANES), F32)
    send, sums0, wide, d_other = call(
        part(first_kernel, tiles), "first", (to_swap, table, lanes, part_half), [VMEM] * 4, [padded, coeffs, field],
        mib=mib, cost=(work, 0),
    )(ens, acc, d_other, share)
    (kept,) = call(part(own_kernel, tiles), "own", (part_half,), [VMEM] * 2, mib=mib, cost=(work, 0))(ens, wide)
    got = exchange((kept + swap(send).astype(F32)).astype(BF16).reshape(to_all.shape))

    q, sent = call(part(middle_kernel, tiles), "middle", (mine, to_all), [VMEM] * 3)(got, direct, obs)
    p_mine = exchange(sent).reshape(half, LANES)
    p_other = swap(p_mine)

    small = shape((8, LANES), F32)
    acc, dd, pd, pp = call(
        part(own_sums_kernel, tiles), "sums", (table, table, table, table), [VMEM] * 4, [field], mib=mib, cost=(work, 0)
    )(ens, p_mine, d_mine, d_other)
    send, wide, scal, sums, coeff = call(
        part(second_kernel, tiles),
        "second",
        (to_swap, lanes, small, table, table),
        [VMEM] * 9,
        [field, coeffs, coeffs, padded, field],
        mib=mib,
        cost=(work, 0),
    )(ens, acc, dd, pd, pp, d_other, p_other, share, sums0)
    kept, extra = call(
        part(second_own_kernel, tiles), "second_own", (part_half, small), [VMEM] * 8, mib=mib, cost=(work, 0)
    )(ens, wide, sums, coeff, scal, direct, q, obs)
    both = (kept + swap(send).astype(F32)).reshape(to_all.shape)
    both = jnp.concatenate([both, jnp.broadcast_to(extra[None], (devices, 8, LANES))], axis=1)
    got = exchange(both.astype(BF16))
    out = shape((own, cells), F32)
    scratch = pltpu.VMEM((2 * rows, LANES), F32)
    return call(part(last_kernel, tiles), "last", (out, out), [VMEM] * 5, [scratch] * 2)(got, scal, direct, obs, q)


def solution(mesh):
    return jax.shard_map(
        per_device,
        mesh=mesh,
        in_specs=(
            P(AXES, None, None),
            P(AXES, None),
            P(AXES, None),
            P(),
            P(),
        ),
        out_specs=(P(AXES, None), P(AXES, None)),
        check_vma=False,
    )
```

```python
import functools

import jax
import jax.numpy as jnp
from jax import lax
from jax.experimental import pallas as pl
from jax.experimental.pallas import tpu as pltpu
from jax.sharding import PartitionSpec as P

AXES = ("mem", "grid")
M = 1024
LANES = 128
ROWS = 16
KEEP = 0.125
REACH = 3
SHIFTS = range(-REACH, REACH + 1)
F32 = jnp.float32
BF16 = jnp.bfloat16
VMEM = pl.BlockSpec(memory_space=pltpu.VMEM)
HBM = pl.BlockSpec(memory_space=pltpu.HBM)


def core_index():
    return lax.rem(lax.axis_index("grid"), 2)


def every(ref, t, first, blocks, tiles):
    return ref[pl.ds(first * tiles + t, blocks, stride=tiles), :]


def lay_kernel(tiles, field_ref, halves_ref):
    own = field_ref.shape[0]
    for h in range(2):
        for t in range(tiles):
            cells = pl.ds((h * tiles + t) * LANES, LANES)
            halves_ref[pl.ds(h * own * tiles + t, own, stride=tiles), :] = field_ref[:, cells]


def start_kernel(tiles, right_ref, sent_ref, direct_ref):
    lay_kernel(tiles, right_ref, direct_ref)
    spread_out(direct_ref[...].astype(BF16), sent_ref)


def spread_out(both, sent_ref):
    devices, rows, _ = sent_ref.shape
    low, high = both[:rows], both[rows:]
    for chip in range(devices // 2):
        sent_ref[2 * chip] = low
        sent_ref[2 * chip + 1] = high


def load_kernel(
    tiles, ens_hbm, nbr_hbm, weight_hbm, obs_hbm, mine_ref, ens_ref, share_ref, acc_ref, obs_ref, mine,
    held, nbr_ref, weight_ref, laid, sems, small,
):
    members, blocks, cells = ens_hbm.shape
    half = cells // 2
    core = core_index()
    each = sems.shape[1]
    chunks, each = each, members // each

    def copies(c):
        span = pl.ds(c * each, each)
        out = []
        for slot in range(2):
            col = pl.multiple_of(lax.rem(core + slot, 2) * half, half)
            source = ens_hbm.at[span, :, pl.ds(col, half)]
            out.append(pltpu.make_async_copy(source, held.at[slot, span], sems.at[slot, c]))
        return out

    lists = (
        pltpu.make_async_copy(nbr_hbm, nbr_ref, small.at[0]),
        pltpu.make_async_copy(weight_hbm, weight_ref, small.at[1]),
        pltpu.make_async_copy(obs_hbm, laid, small.at[2]),
    )
    for copy in lists:
        copy.start()

    def begin(c, _):
        for copy in copies(c):
            copy.start()
        return 0

    lax.fori_loop(0, chunks, begin, 0)
    mine[...] = mine_ref[...].astype(F32)
    for copy in lists:
        copy.wait()
    lay_kernel(tiles, laid, obs_ref)
    away = nbr_ref[...] - lax.broadcasted_iota(jnp.int32, nbr_ref.shape, 1)
    away = jnp.where(away > blocks // 2, away - blocks, away)
    away = jnp.where(away < -(blocks // 2), away + blocks, away)
    row = lax.broadcasted_iota(jnp.int32, (8, blocks), 0)
    shares = jnp.zeros((8, blocks), F32)
    for i, shift in enumerate(SHIFTS):
        share = jnp.sum(jnp.where(away == shift, weight_ref[...], 0.0), axis=0, keepdims=True)
        shares = jnp.where(row == i, share, shares)
    shares = shares.T
    for i in range(len(SHIFTS)):
        share_ref[i] = jnp.broadcast_to(shares[:, i : i + 1], (blocks, LANES))

    acc_ref[...] = jnp.zeros_like(acc_ref)
    lane = lax.broadcasted_iota(jnp.int32, (ROWS, LANES), 1)

    def chunk(c, _):
        for copy in copies(c):
            copy.wait()

        def body(first):
            here = pl.ds(first, ROWS)
            parts = [every(mine, t, first, ROWS, tiles) for t in range(tiles)]
            sums = acc_ref[here, :]
            for i in range(each):
                k = c * each + i
                acc = None
                for t in range(tiles):
                    cells = pl.ds(t * LANES, LANES)
                    one = held[0, k, here, cells].astype(F32)
                    ens_ref[0, k, here, cells] = one
                    acc = one * parts[t] if acc is None else acc + one * parts[t]
                sums = jnp.where(lane == k, jnp.sum(acc, axis=1, keepdims=True), sums)
                for t in range(tiles):
                    cells = pl.ds(t * LANES, LANES)
                    ens_ref[1, k, here, cells] = held[1, k, here, cells].astype(F32)
            acc_ref[here, :] = sums

        groups(blocks, ROWS, 8, body)
        return 0

    lax.fori_loop(0, chunks, chunk, 0)


def groups(blocks, rows, unroll, body):
    def group(g, _):
        body(g * rows if isinstance(g, int) else pl.multiple_of(g * rows, rows))
        return 0

    lax.fori_loop(0, blocks // rows, group, 0, unroll=unroll)


def own_sums_kernel(tiles, ens_ref, mine_ref, dm_ref, do_ref, acc_ref, dd_ref, pd_ref, pp_ref, mine):
    blocks = ens_ref.shape[2]
    mine[...] = mine_ref[...].astype(F32)

    half_sums(ens_ref, 0, mine, acc_ref, tiles)

    def body(first):
        here = pl.ds(first, 8)
        parts = [every(mine, t, first, 8, tiles) for t in range(tiles)]
        own = [every(dm_ref, t, first, 8, tiles) for t in range(tiles)]
        far = [every(do_ref, t, first, 8, tiles) for t in range(tiles)]
        dd_ref[here, :] = sum(d * d for d in own + far)
        pd_ref[here, :] = sum(p * d for p, d in zip(parts, own))
        pp_ref[here, :] = sum(p * p for p in parts)

    groups(blocks, 8, 16, body)


def half_sums(ens_ref, slot, field, sums_ref, tiles, start=None):
    _, members, blocks, _ = ens_ref.shape
    lane = lax.broadcasted_iota(jnp.int32, (ROWS, LANES), 1)

    def body(first):
        here = pl.ds(first, ROWS)
        parts = [every(field, t, first, ROWS, tiles) for t in range(tiles)]
        out = jnp.zeros((ROWS, LANES), F32)
        for k in range(members):
            acc = None
            for t in range(tiles):
                term = ens_ref[slot, k, here, pl.ds(t * LANES, LANES)] * parts[t]
                acc = term if acc is None else acc + term
            out = jnp.where(lane == k, jnp.sum(acc, axis=1, keepdims=True), out)
        sums_ref[here, :] = out if start is None else out + start[here, :]

    groups(blocks, ROWS, 8, body)


def mixed(sums, pad_ref, share_ref):
    blocks = sums.shape[0]
    pad_ref[pl.ds(8, blocks), :] = sums
    pad_ref[pl.ds(0, 8), :] = sums[blocks - 8 :]
    pad_ref[pl.ds(8 + blocks, 8), :] = sums[:8]
    total = sums
    for i, shift in enumerate(SHIFTS):
        total = total + share_ref[i] * pad_ref[pl.ds(8 + shift, blocks), :]
    return total.astype(BF16).astype(F32)


def half_spread(ens_ref, slot, coeff, wide_ref, out_ref, tiles):
    _, members, blocks, _ = ens_ref.shape
    rows, unroll = (8, 16) if coeff is None else (16, 8)

    def body(first):
        here = None if coeff is None else coeff[pl.ds(first, rows), :]
        acc = [None] * tiles
        for k in range(members):
            if here is None:
                one = wide_ref[k, pl.ds(first, rows), :]
            else:
                one = jnp.broadcast_to(here[:, k : k + 1].astype(BF16), (rows, LANES)).astype(F32)
                wide_ref[k, pl.ds(first, rows), :] = one
            for t in range(tiles):
                term = ens_ref[slot, k, pl.ds(first, rows), pl.ds(t * LANES, LANES)] * one
                acc[t] = term if acc[t] is None else acc[t] + term
        for t in range(tiles):
            out_ref[pl.ds(first * tiles + t, rows, stride=tiles), :] = acc[t]

    groups(blocks, rows, unroll, body)


def first_kernel(tiles, ens_ref, acc_ref, other_ref, share_ref, send_ref, sums_ref, wide_ref, other, pad_ref, coeff_ref, spread):
    other[...] = other_ref[...].astype(F32)
    half_sums(ens_ref, 1, other, sums_ref, tiles, acc_ref)
    coeff_ref[...] = mixed(sums_ref[...], pad_ref, share_ref)
    half_spread(ens_ref, 1, coeff_ref, wide_ref, spread, tiles)
    send_ref[...] = spread[...].astype(BF16)


def own_kernel(tiles, ens_ref, wide_ref, own_ref):
    half_spread(ens_ref, 0, None, wide_ref, own_ref, tiles)


def received(got, rows):
    devices = got.shape[0]
    sums = []
    for core in range(2):
        total = None
        for chip in range(devices // 2):
            one = got[2 * chip + core, :rows, :].astype(F32)
            total = one if total is None else total + one
        sums.append(total)
    return jnp.concatenate(sums, axis=0)


def middle_kernel(tiles, got_ref, direct_ref, obs_ref, q_ref, sent_ref):
    _, rows, _ = got_ref.shape
    direct = direct_ref[...]
    q = obs_ref[...] * direct + received(got_ref, rows) * (1.0 / M)
    q_ref[...] = q
    d = direct.astype(BF16).astype(F32)
    dd = jnp.sum(direct * d, axis=1, keepdims=True)
    qd = jnp.sum(d * q, axis=1, keepdims=True)
    row = lax.broadcasted_iota(jnp.int32, dd.shape, 0) % rows // tiles
    tau = jnp.zeros_like(dd)
    for b in range(rows // tiles):
        here = row == b
        self = jnp.sum(jnp.where(here, dd, 0.0), axis=0, keepdims=True)
        prod = jnp.sum(jnp.where(here, qd, 0.0), axis=0, keepdims=True)
        share = jnp.where(self > 0.0, (1.0 - KEEP) * prod / jnp.where(self > 0.0, self, 1.0), 0.0)
        tau = jnp.where(here, share, tau)
    spread_out((q - tau * direct).astype(BF16), sent_ref)


def second_kernel(
    tiles, ens_ref, acc_ref, dd_ref, pd_ref, pp_ref, do_ref, po_ref, share_ref, sums0_ref,
    send_ref, wide_ref, scal_ref, sums_ref, coeff_ref, other, pd_all, pp_all, pad_ref, spread,
):
    blocks = ens_ref.shape[2]
    other[...] = po_ref[...].astype(F32)

    def products(first):
        here = pl.ds(first, ROWS)
        parts = [every(other, t, first, ROWS, tiles) for t in range(tiles)]
        far = [every(do_ref, t, first, ROWS, tiles) for t in range(tiles)]
        pd_all[here, :] = pd_ref[here, :] + sum(p * d for p, d in zip(parts, far))
        pp_all[here, :] = pp_ref[here, :] + sum(p * p for p in parts)

    groups(blocks, ROWS, 8, products)
    dd = jnp.sum(dd_ref[...], axis=1, keepdims=True)
    pd = jnp.sum(pd_all[...], axis=1, keepdims=True)
    pp = jnp.sum(pp_all[...], axis=1, keepdims=True)
    tau = jnp.where(dd > 0.0, (1.0 / KEEP - 1.0) * pd / jnp.where(dd > 0.0, dd, 1.0), 0.0)
    rr0 = jnp.sum(dd, axis=0, keepdims=True)
    alpha = rr0 / jnp.sum(pd + tau * dd, axis=0, keepdims=True)
    keep = 1.0 - alpha * tau
    rr1 = jnp.sum(keep * (keep * dd - 2.0 * alpha * pd) + alpha * alpha * pp, axis=0, keepdims=True)
    beta = rr1 / rr0
    row = lax.broadcasted_iota(jnp.int32, (8, LANES), 0)
    scal_ref[...] = jnp.where(row == 0, alpha, jnp.where(row == 1, beta, rr1))
    half_sums(ens_ref, 1, other, sums_ref, tiles, acc_ref)
    sums = (beta + keep) * sums0_ref[...] - alpha * sums_ref[...]
    sums_ref[...] = sums
    coeff_ref[...] = mixed(sums, pad_ref, share_ref)
    half_spread(ens_ref, 1, coeff_ref, wide_ref, spread, tiles)
    send_ref[...] = spread[...].astype(BF16)


def second_own_kernel(
    tiles, ens_ref, wide_ref, sums_ref, coeff_ref, scal_ref, direct_ref, q_ref, obs_ref, own_ref, extra_ref
):
    alpha, beta = scal_ref[0:1, :], scal_ref[1:2, :]
    direction = (1.0 + beta) * direct_ref[...] - alpha * q_ref[...]
    part = jnp.sum(jnp.sum(sums_ref[...] * coeff_ref[...], axis=0, keepdims=True), axis=1, keepdims=True) * (1.0 / M)
    part += jnp.sum(jnp.sum(obs_ref[...] * direction * direction, axis=0, keepdims=True), axis=1, keepdims=True)
    row = lax.broadcasted_iota(jnp.int32, (8, LANES), 0)
    lane = lax.broadcasted_iota(jnp.int32, (8, LANES), 1)
    high = part.astype(BF16).astype(F32)
    mid = (part - high).astype(BF16).astype(F32)
    extra_ref[...] = jnp.where(row == 0, jnp.where(lane < LANES // 2, high, mid), part - high - mid)
    half_spread(ens_ref, 0, None, wide_ref, own_ref, tiles)


def last_kernel(tiles, spread_ref, extra_ref, scal_ref, direct_ref, obs_ref, q_ref, solution_ref, residual_ref, sol, res):
    rows = spread_ref.shape[0] // 2
    parts = extra_ref[0] + extra_ref[1]
    denom = jnp.sum(parts[0:1], axis=1, keepdims=True) * (2.0 / LANES) + parts[1:2]
    alpha, beta, rr1 = scal_ref[0:1, :], scal_ref[1:2, :], scal_ref[2:3, :]
    direct = direct_ref[...]
    residual = direct - alpha * q_ref[...]
    direction = residual + beta * direct
    image = obs_ref[...] * direction + spread_ref[...] * (1.0 / M)
    alpha1 = rr1 / denom
    sol[...] = alpha * direct + alpha1 * direction
    res[...] = residual - alpha1 * image
    own = solution_ref.shape[0]
    for h in range(2):
        for t in range(tiles):
            cells = pl.ds((h * tiles + t) * LANES, LANES)
            at = pl.ds(h * rows + t, own, stride=tiles)
            solution_ref[:, cells] = sol[at, :]
            residual_ref[:, cells] = res[at, :]


def call(kernel, name, outs, ins, scratch=(), mib=8, cost=(0, 0)):
    return pl.pallas_call(
        kernel,
        name=name,
        out_shape=tuple(outs),
        in_specs=ins,
        out_specs=(VMEM,) * len(outs),
        scratch_shapes=list(scratch),
        compiler_params=pltpu.CompilerParams(vmem_limit_bytes=mib * 1024 * 1024),
        cost_estimate=pl.CostEstimate(flops=cost[0], bytes_accessed=cost[1], transcendentals=0),
    )


def per_device(ensemble, right_side, obs_prec, neighbors, loc_weight):
    own, cells = right_side.shape
    members, blocks, _ = ensemble.shape
    devices = lax.axis_size(AXES)
    tiles = cells // (2 * LANES)
    rows = own * tiles
    half = blocks * tiles
    pairs = [(i, i ^ 1) for i in range(devices)]
    shape = jax.ShapeDtypeStruct
    part = functools.partial
    mib = 4 + 4 * blocks // 128

    def swap(x):
        return lax.ppermute(x, AXES, pairs)

    def exchange(x):
        return lax.all_to_all(x, AXES, split_axis=0, concat_axis=0, tiled=True)

    to_all = shape((devices, rows, LANES), BF16)
    lanes = shape((members, blocks, LANES), F32)
    table = shape((blocks, LANES), F32)
    to_swap = shape((half, LANES), BF16)
    part_half = shape((half, LANES), F32)
    mine = shape((2 * rows, LANES), F32)
    field = pltpu.VMEM((half, LANES), F32)
    padded = pltpu.VMEM((blocks + 16, LANES), F32)
    work = 2 * members * blocks * cells

    sent, direct = call(part(start_kernel, tiles), "start", (to_all, mine), [VMEM])(right_side)
    d_mine = exchange(sent).reshape(half, LANES)
    d_other = swap(d_mine)
    ens, share, acc, obs, d_mine = call(
        part(load_kernel, tiles),
        "load",
        (shape((2, members, blocks, cells // 2), F32), shape((len(SHIFTS), blocks, LANES), F32), table, mine, part_half),
        [HBM, HBM, HBM, HBM, VMEM],
        [
            pltpu.VMEM((2, members, blocks, cells // 2), BF16),
            pltpu.VMEM(neighbors.shape[::-1], jnp.int32),
            pltpu.VMEM(loc_weight.shape[::-1], F32),
            pltpu.VMEM((own, cells), F32),
            pltpu.SemaphoreType.DMA((2, members // 4)),
            pltpu.SemaphoreType.DMA((3,)),
        ],
        mib=8 + mib,
        cost=(work, 6 * members * blocks * cells),
    )(*(pltpu.with_memory_space_constraint(x, pltpu.HBM) for x in (ensemble, neighbors.T, loc_weight.T, obs_prec)), d_mine)

    coeffs = pltpu.VMEM((blocks, LANES), F32)
    send, sums0, wide, d_other = call(
        part(first_kernel, tiles), "first", (to_swap, table, lanes, part_half), [VMEM] * 4, [padded, coeffs, field],
        mib=mib, cost=(work, 0),
    )(ens, acc, d_other, share)
    (kept,) = call(part(own_kernel, tiles), "own", (part_half,), [VMEM] * 2, mib=mib, cost=(work, 0))(ens, wide)
    got = exchange((kept + swap(send).astype(F32)).astype(BF16).reshape(to_all.shape))

    q, sent = call(part(middle_kernel, tiles), "middle", (mine, to_all), [VMEM] * 3)(got, direct, obs)
    p_mine = exchange(sent).reshape(half, LANES)
    p_other = swap(p_mine)

    small = shape((8, LANES), F32)
    acc, dd, pd, pp = call(
        part(own_sums_kernel, tiles), "sums", (table, table, table, table), [VMEM] * 4, [field], mib=mib, cost=(work, 0)
    )(ens, p_mine, d_mine, d_other)
    send, wide, scal, sums, coeff = call(
        part(second_kernel, tiles),
        "second",
        (to_swap, lanes, small, table, table),
        [VMEM] * 9,
        [field, coeffs, coeffs, padded, field],
        mib=mib,
        cost=(work, 0),
    )(ens, acc, dd, pd, pp, d_other, p_other, share, sums0)
    kept, extra = call(
        part(second_own_kernel, tiles), "second_own", (part_half, small), [VMEM] * 8, mib=mib, cost=(work, 0)
    )(ens, wide, sums, coeff, scal, direct, q, obs)
    both = (kept + swap(send).astype(F32)).astype(BF16).reshape(devices, rows // 2, 2, LANES)
    extra = jnp.broadcast_to(extra[:2].astype(BF16).reshape(1, 1, 2, LANES), (devices, 1, 2, LANES))
    got = exchange(jnp.concatenate([both, extra], axis=1))
    got = jnp.sum(got.reshape(devices // 2, 2, rows // 2 + 1, 2, LANES).astype(F32), axis=0)
    spread = got[:, : rows // 2].reshape(2 * rows, LANES)
    extra = got[:, rows // 2]
    out = shape((own, cells), F32)
    scratch = pltpu.VMEM((2 * rows, LANES), F32)
    return call(part(last_kernel, tiles), "last", (out, out), [VMEM] * 6, [scratch] * 2)(spread, extra, scal, direct, obs, q)


def solution(mesh):
    return jax.shard_map(
        per_device,
        mesh=mesh,
        in_specs=(
            P(AXES, None, None),
            P(AXES, None),
            P(AXES, None),
            P(),
            P(),
        ),
        out_specs=(P(AXES, None), P(AXES, None)),
        check_vma=False,
    )
```

```python
import functools

import jax
import jax.numpy as jnp
from jax import lax
from jax.experimental import pallas as pl
from jax.experimental.pallas import tpu as pltpu
from jax.sharding import PartitionSpec as P

AXES = ("mem", "grid")
M = 1024
LANES = 128
ROWS = 16
KEEP = 0.125
REACH = 3
SHIFTS = range(-REACH, REACH + 1)
F32 = jnp.float32
BF16 = jnp.bfloat16
VMEM = pl.BlockSpec(memory_space=pltpu.VMEM)
HBM = pl.BlockSpec(memory_space=pltpu.HBM)


def core_index():
    return lax.rem(lax.axis_index("grid"), 2)


def every(ref, t, first, blocks, tiles):
    return ref[pl.ds(first * tiles + t, blocks, stride=tiles), :]


def lay_kernel(tiles, field_ref, halves_ref):
    own = field_ref.shape[0]
    for h in range(2):
        for t in range(tiles):
            cells = pl.ds((h * tiles + t) * LANES, LANES)
            halves_ref[pl.ds(h * own * tiles + t, own, stride=tiles), :] = field_ref[:, cells]


def start_kernel(tiles, right_ref, sent_ref, direct_ref):
    lay_kernel(tiles, right_ref, direct_ref)
    spread_out(direct_ref[...].astype(BF16), sent_ref)


def spread_out(both, sent_ref):
    devices, rows, _ = sent_ref.shape
    low, high = both[:rows], both[rows:]
    for chip in range(devices // 2):
        sent_ref[2 * chip] = low
        sent_ref[2 * chip + 1] = high


def load_kernel(
    tiles, ens_hbm, nbr_hbm, weight_hbm, obs_hbm, mine_ref, ens_ref, share_ref, acc_ref, obs_ref, mine,
    held, nbr_ref, weight_ref, laid, sems, small,
):
    members, blocks, cells = ens_hbm.shape
    half = cells // 2
    core = core_index()
    each = sems.shape[1]
    chunks, each = each, members // each

    def copies(c):
        span = pl.ds(c * each, each)
        out = []
        for slot in range(2):
            col = pl.multiple_of(lax.rem(core + slot, 2) * half, half)
            source = ens_hbm.at[span, :, pl.ds(col, half)]
            out.append(pltpu.make_async_copy(source, held.at[slot, span], sems.at[slot, c]))
        return out

    lists = (
        pltpu.make_async_copy(nbr_hbm, nbr_ref, small.at[0]),
        pltpu.make_async_copy(weight_hbm, weight_ref, small.at[1]),
        pltpu.make_async_copy(obs_hbm, laid, small.at[2]),
    )
    for copy in lists:
        copy.start()

    def begin(c, _):
        for copy in copies(c):
            copy.start()
        return 0

    lax.fori_loop(0, chunks, begin, 0)
    mine[...] = mine_ref[...].astype(F32)
    for copy in lists:
        copy.wait()
    lay_kernel(tiles, laid, obs_ref)
    away = nbr_ref[...] - lax.broadcasted_iota(jnp.int32, nbr_ref.shape, 1)
    away = jnp.where(away > blocks // 2, away - blocks, away)
    away = jnp.where(away < -(blocks // 2), away + blocks, away)
    row = lax.broadcasted_iota(jnp.int32, (8, blocks), 0)
    shares = jnp.zeros((8, blocks), F32)
    for i, shift in enumerate(SHIFTS):
        share = jnp.sum(jnp.where(away == shift, weight_ref[...], 0.0), axis=0, keepdims=True)
        shares = jnp.where(row == i, share, shares)
    shares = shares.T
    for i in range(len(SHIFTS)):
        share_ref[i] = jnp.broadcast_to(shares[:, i : i + 1], (blocks, LANES))

    acc_ref[...] = jnp.zeros_like(acc_ref)
    lane = lax.broadcasted_iota(jnp.int32, (ROWS, LANES), 1)

    def chunk(c, _):
        for copy in copies(c):
            copy.wait()

        def body(first):
            here = pl.ds(first, ROWS)
            parts = [every(mine, t, first, ROWS, tiles) for t in range(tiles)]
            sums = acc_ref[here, :]
            for i in range(each):
                k = c * each + i
                acc = None
                for t in range(tiles):
                    cells = pl.ds(t * LANES, LANES)
                    one = held[0, k, here, cells].astype(F32)
                    ens_ref[0, k, here, cells] = one
                    acc = one * parts[t] if acc is None else acc + one * parts[t]
                sums = jnp.where(lane == k, jnp.sum(acc, axis=1, keepdims=True), sums)
                for t in range(tiles):
                    cells = pl.ds(t * LANES, LANES)
                    ens_ref[1, k, here, cells] = held[1, k, here, cells].astype(F32)
            acc_ref[here, :] = sums

        groups(blocks, ROWS, 8, body)
        return 0

    lax.fori_loop(0, chunks, chunk, 0)


def groups(blocks, rows, unroll, body):
    def group(g, _):
        body(g * rows if isinstance(g, int) else pl.multiple_of(g * rows, rows))
        return 0

    lax.fori_loop(0, blocks // rows, group, 0, unroll=unroll)


def own_sums_kernel(tiles, ens_ref, mine_ref, dm_ref, do_ref, acc_ref, dd_ref, pd_ref, pp_ref, mine):
    blocks = ens_ref.shape[2]
    mine[...] = mine_ref[...].astype(F32)

    half_sums(ens_ref, 0, mine, acc_ref, tiles)

    def body(first):
        here = pl.ds(first, 8)
        parts = [every(mine, t, first, 8, tiles) for t in range(tiles)]
        own = [every(dm_ref, t, first, 8, tiles) for t in range(tiles)]
        far = [every(do_ref, t, first, 8, tiles) for t in range(tiles)]
        dd_ref[here, :] = sum(d * d for d in own + far)
        pd_ref[here, :] = sum(p * d for p, d in zip(parts, own))
        pp_ref[here, :] = sum(p * p for p in parts)

    groups(blocks, 8, 16, body)


def half_sums(ens_ref, slot, field, sums_ref, tiles, start=None):
    _, members, blocks, _ = ens_ref.shape
    lane = lax.broadcasted_iota(jnp.int32, (ROWS, LANES), 1)

    def body(first):
        here = pl.ds(first, ROWS)
        parts = [every(field, t, first, ROWS, tiles) for t in range(tiles)]
        out = jnp.zeros((ROWS, LANES), F32)
        for k in range(members):
            acc = None
            for t in range(tiles):
                term = ens_ref[slot, k, here, pl.ds(t * LANES, LANES)] * parts[t]
                acc = term if acc is None else acc + term
            out = jnp.where(lane == k, jnp.sum(acc, axis=1, keepdims=True), out)
        sums_ref[here, :] = out if start is None else out + start[here, :]

    groups(blocks, ROWS, 8, body)


def mixed(sums, pad_ref, share_ref):
    blocks = sums.shape[0]
    pad_ref[pl.ds(8, blocks), :] = sums
    pad_ref[pl.ds(0, 8), :] = sums[blocks - 8 :]
    pad_ref[pl.ds(8 + blocks, 8), :] = sums[:8]
    total = sums
    for i, shift in enumerate(SHIFTS):
        total = total + share_ref[i] * pad_ref[pl.ds(8 + shift, blocks), :]
    return total.astype(BF16).astype(F32)


def half_spread(ens_ref, slot, coeff, wide_ref, out_ref, tiles, send_ref=None):
    _, members, blocks, _ = ens_ref.shape
    rows, unroll = (8, 16) if coeff is None else (16, 8)

    def body(first):
        here = None if coeff is None else coeff[pl.ds(first, rows), :]
        acc = [None] * tiles
        for k in range(members):
            if here is None:
                one = wide_ref[k, pl.ds(first, rows), :]
            else:
                one = jnp.broadcast_to(here[:, k : k + 1].astype(BF16), (rows, LANES)).astype(F32)
                wide_ref[k, pl.ds(first, rows), :] = one
            for t in range(tiles):
                term = ens_ref[slot, k, pl.ds(first, rows), pl.ds(t * LANES, LANES)] * one
                acc[t] = term if acc[t] is None else acc[t] + term
        for t in range(tiles):
            out_ref[pl.ds(first * tiles + t, rows, stride=tiles), :] = acc[t]
        if send_ref is not None:
            span = pl.ds(first * tiles, rows * tiles)
            send_ref[span, :] = out_ref[span, :].astype(BF16)

    groups(blocks, rows, unroll, body)


def first_kernel(tiles, ens_ref, acc_ref, other_ref, share_ref, send_ref, sums_ref, wide_ref, other, pad_ref, coeff_ref, spread):
    other[...] = other_ref[...].astype(F32)
    half_sums(ens_ref, 1, other, sums_ref, tiles, acc_ref)
    coeff_ref[...] = mixed(sums_ref[...], pad_ref, share_ref)
    half_spread(ens_ref, 1, coeff_ref, wide_ref, spread, tiles, send_ref)


def own_kernel(tiles, ens_ref, wide_ref, own_ref):
    half_spread(ens_ref, 0, None, wide_ref, own_ref, tiles)


def received(got, rows):
    devices = got.shape[0]
    sums = []
    for core in range(2):
        total = None
        for chip in range(devices // 2):
            one = got[2 * chip + core, :rows, :].astype(F32)
            total = one if total is None else total + one
        sums.append(total)
    return jnp.concatenate(sums, axis=0)


def middle_kernel(tiles, got_ref, direct_ref, obs_ref, q_ref, sent_ref):
    _, rows, _ = got_ref.shape
    direct = direct_ref[...]
    q = obs_ref[...] * direct + received(got_ref, rows) * (1.0 / M)
    q_ref[...] = q
    d = direct.astype(BF16).astype(F32)
    dd = jnp.sum(direct * d, axis=1, keepdims=True)
    qd = jnp.sum(d * q, axis=1, keepdims=True)
    row = lax.broadcasted_iota(jnp.int32, dd.shape, 0) % rows // tiles
    tau = jnp.zeros_like(dd)
    for b in range(rows // tiles):
        here = row == b
        self = jnp.sum(jnp.where(here, dd, 0.0), axis=0, keepdims=True)
        prod = jnp.sum(jnp.where(here, qd, 0.0), axis=0, keepdims=True)
        share = jnp.where(self > 0.0, (1.0 - KEEP) * prod / jnp.where(self > 0.0, self, 1.0), 0.0)
        tau = jnp.where(here, share, tau)
    spread_out((q - tau * direct).astype(BF16), sent_ref)


def second_kernel(
    tiles, ens_ref, acc_ref, dd_ref, pd_ref, pp_ref, do_ref, po_ref, share_ref, sums0_ref,
    send_ref, wide_ref, scal_ref, sums_ref, coeff_ref, other, pd_all, pp_all, pad_ref, spread,
):
    blocks = ens_ref.shape[2]
    other[...] = po_ref[...].astype(F32)

    def products(first):
        here = pl.ds(first, ROWS)
        parts = [every(other, t, first, ROWS, tiles) for t in range(tiles)]
        far = [every(do_ref, t, first, ROWS, tiles) for t in range(tiles)]
        pd_all[here, :] = pd_ref[here, :] + sum(p * d for p, d in zip(parts, far))
        pp_all[here, :] = pp_ref[here, :] + sum(p * p for p in parts)

    groups(blocks, ROWS, 8, products)
    dd = jnp.sum(dd_ref[...], axis=1, keepdims=True)
    pd = jnp.sum(pd_all[...], axis=1, keepdims=True)
    pp = jnp.sum(pp_all[...], axis=1, keepdims=True)
    tau = jnp.where(dd > 0.0, (1.0 / KEEP - 1.0) * pd / jnp.where(dd > 0.0, dd, 1.0), 0.0)
    rr0 = jnp.sum(dd, axis=0, keepdims=True)
    alpha = rr0 / jnp.sum(pd + tau * dd, axis=0, keepdims=True)
    keep = 1.0 - alpha * tau
    rr1 = jnp.sum(keep * (keep * dd - 2.0 * alpha * pd) + alpha * alpha * pp, axis=0, keepdims=True)
    beta = rr1 / rr0
    row = lax.broadcasted_iota(jnp.int32, (8, LANES), 0)
    scal_ref[...] = jnp.where(row == 0, alpha, jnp.where(row == 1, beta, rr1))
    half_sums(ens_ref, 1, other, sums_ref, tiles, acc_ref)
    sums = (beta + keep) * sums0_ref[...] - alpha * sums_ref[...]
    sums_ref[...] = sums
    coeff_ref[...] = mixed(sums, pad_ref, share_ref)
    half_spread(ens_ref, 1, coeff_ref, wide_ref, spread, tiles, send_ref)


def second_own_kernel(
    tiles, ens_ref, wide_ref, sums_ref, coeff_ref, scal_ref, direct_ref, q_ref, obs_ref, own_ref, extra_ref
):
    alpha, beta = scal_ref[0:1, :], scal_ref[1:2, :]
    direction = (1.0 + beta) * direct_ref[...] - alpha * q_ref[...]
    part = jnp.sum(jnp.sum(sums_ref[...] * coeff_ref[...], axis=0, keepdims=True), axis=1, keepdims=True) * (1.0 / M)
    part += jnp.sum(jnp.sum(obs_ref[...] * direction * direction, axis=0, keepdims=True), axis=1, keepdims=True)
    row = lax.broadcasted_iota(jnp.int32, (8, LANES), 0)
    lane = lax.broadcasted_iota(jnp.int32, (8, LANES), 1)
    high = part.astype(BF16).astype(F32)
    mid = (part - high).astype(BF16).astype(F32)
    extra_ref[...] = jnp.where(row == 0, jnp.where(lane < LANES // 2, high, mid), part - high - mid)
    half_spread(ens_ref, 0, None, wide_ref, own_ref, tiles)


def last_kernel(tiles, spread_ref, extra_ref, scal_ref, direct_ref, obs_ref, q_ref, solution_ref, residual_ref, sol, res):
    rows = spread_ref.shape[0] // 2
    parts = extra_ref[0] + extra_ref[1]
    denom = jnp.sum(parts[0:1], axis=1, keepdims=True) * (2.0 / LANES) + parts[1:2]
    alpha, beta, rr1 = scal_ref[0:1, :], scal_ref[1:2, :], scal_ref[2:3, :]
    direct = direct_ref[...]
    residual = direct - alpha * q_ref[...]
    direction = residual + beta * direct
    image = obs_ref[...] * direction + spread_ref[...] * (1.0 / M)
    alpha1 = rr1 / denom
    sol[...] = alpha * direct + alpha1 * direction
    res[...] = residual - alpha1 * image
    own = solution_ref.shape[0]
    for h in range(2):
        for t in range(tiles):
            cells = pl.ds((h * tiles + t) * LANES, LANES)
            at = pl.ds(h * rows + t, own, stride=tiles)
            solution_ref[:, cells] = sol[at, :]
            residual_ref[:, cells] = res[at, :]


def call(kernel, name, outs, ins, scratch=(), mib=8, cost=(0, 0)):
    return pl.pallas_call(
        kernel,
        name=name,
        out_shape=tuple(outs),
        in_specs=ins,
        out_specs=(VMEM,) * len(outs),
        scratch_shapes=list(scratch),
        compiler_params=pltpu.CompilerParams(vmem_limit_bytes=mib * 1024 * 1024),
        cost_estimate=pl.CostEstimate(flops=cost[0], bytes_accessed=cost[1], transcendentals=0),
    )


def per_device(ensemble, right_side, obs_prec, neighbors, loc_weight):
    own, cells = right_side.shape
    members, blocks, _ = ensemble.shape
    devices = lax.axis_size(AXES)
    tiles = cells // (2 * LANES)
    rows = own * tiles
    half = blocks * tiles
    pairs = [(i, i ^ 1) for i in range(devices)]
    shape = jax.ShapeDtypeStruct
    part = functools.partial
    mib = 4 + 4 * blocks // 128

    def swap(x):
        return lax.ppermute(x, AXES, pairs)

    def exchange(x):
        return lax.all_to_all(x, AXES, split_axis=0, concat_axis=0, tiled=True)

    to_all = shape((devices, rows, LANES), BF16)
    lanes = shape((members, blocks, LANES), F32)
    table = shape((blocks, LANES), F32)
    to_swap = shape((half, LANES), BF16)
    part_half = shape((half, LANES), F32)
    mine = shape((2 * rows, LANES), F32)
    field = pltpu.VMEM((half, LANES), F32)
    padded = pltpu.VMEM((blocks + 16, LANES), F32)
    work = 2 * members * blocks * cells

    sent, direct = call(part(start_kernel, tiles), "start", (to_all, mine), [VMEM])(right_side)
    d_mine = exchange(sent).reshape(half, LANES)
    d_other = swap(d_mine)
    ens, share, acc, obs, d_mine = call(
        part(load_kernel, tiles),
        "load",
        (shape((2, members, blocks, cells // 2), F32), shape((len(SHIFTS), blocks, LANES), F32), table, mine, part_half),
        [HBM, HBM, HBM, HBM, VMEM],
        [
            pltpu.VMEM((2, members, blocks, cells // 2), BF16),
            pltpu.VMEM(neighbors.shape[::-1], jnp.int32),
            pltpu.VMEM(loc_weight.shape[::-1], F32),
            pltpu.VMEM((own, cells), F32),
            pltpu.SemaphoreType.DMA((2, members // 4)),
            pltpu.SemaphoreType.DMA((3,)),
        ],
        mib=8 + mib,
        cost=(work, 6 * members * blocks * cells),
    )(*(pltpu.with_memory_space_constraint(x, pltpu.HBM) for x in (ensemble, neighbors.T, loc_weight.T, obs_prec)), d_mine)

    coeffs = pltpu.VMEM((blocks, LANES), F32)
    send, sums0, wide, d_other = call(
        part(first_kernel, tiles), "first", (to_swap, table, lanes, part_half), [VMEM] * 4, [padded, coeffs, field],
        mib=mib, cost=(work, 0),
    )(ens, acc, d_other, share)
    (kept,) = call(part(own_kernel, tiles), "own", (part_half,), [VMEM] * 2, mib=mib, cost=(work, 0))(ens, wide)
    got = exchange((kept + swap(send).astype(F32)).astype(BF16).reshape(to_all.shape))

    q, sent = call(part(middle_kernel, tiles), "middle", (mine, to_all), [VMEM] * 3)(got, direct, obs)
    p_mine = exchange(sent).reshape(half, LANES)
    p_other = swap(p_mine)

    small = shape((8, LANES), F32)
    acc, dd, pd, pp = call(
        part(own_sums_kernel, tiles), "sums", (table, table, table, table), [VMEM] * 4, [field], mib=mib, cost=(work, 0)
    )(ens, p_mine, d_mine, d_other)
    send, wide, scal, sums, coeff = call(
        part(second_kernel, tiles),
        "second",
        (to_swap, lanes, small, table, table),
        [VMEM] * 9,
        [field, coeffs, coeffs, padded, field],
        mib=mib,
        cost=(work, 0),
    )(ens, acc, dd, pd, pp, d_other, p_other, share, sums0)
    kept, extra = call(
        part(second_own_kernel, tiles), "second_own", (part_half, small), [VMEM] * 8, mib=mib, cost=(work, 0)
    )(ens, wide, sums, coeff, scal, direct, q, obs)
    both = (kept + swap(send).astype(F32)).astype(BF16).reshape(devices, rows // 2, 2, LANES)
    extra = jnp.broadcast_to(extra[:2].astype(BF16).reshape(1, 1, 2, LANES), (devices, 1, 2, LANES))
    got = exchange(jnp.concatenate([both, extra], axis=1))
    got = jnp.sum(got.reshape(devices // 2, 2, rows // 2 + 1, 2, LANES).astype(F32), axis=0)
    spread = got[:, : rows // 2].reshape(2 * rows, LANES)
    extra = got[:, rows // 2]
    out = shape((own, cells), F32)
    scratch = pltpu.VMEM((2 * rows, LANES), F32)
    return call(part(last_kernel, tiles), "last", (out, out), [VMEM] * 6, [scratch] * 2)(spread, extra, scal, direct, obs, q)


def solution(mesh):
    return jax.shard_map(
        per_device,
        mesh=mesh,
        in_specs=(
            P(AXES, None, None),
            P(AXES, None),
            P(AXES, None),
            P(),
            P(),
        ),
        out_specs=(P(AXES, None), P(AXES, None)),
        check_vma=False,
    )
```

```python
import functools

import jax
import jax.numpy as jnp
from jax import lax
from jax.experimental import pallas as pl
from jax.experimental.pallas import tpu as pltpu
from jax.sharding import PartitionSpec as P

AXES = ("mem", "grid")
M = 1024
LANES = 128
ROWS = 16
KEEP = 0.125
REACH = 3
SHIFTS = range(-REACH, REACH + 1)
F32 = jnp.float32
BF16 = jnp.bfloat16
VMEM = pl.BlockSpec(memory_space=pltpu.VMEM)
HBM = pl.BlockSpec(memory_space=pltpu.HBM)


def core_index():
    return lax.rem(lax.axis_index("grid"), 2)


def every(ref, t, first, blocks, tiles):
    return ref[pl.ds(first * tiles + t, blocks, stride=tiles), :]


def lay_kernel(tiles, field_ref, halves_ref):
    own = field_ref.shape[0]
    for h in range(2):
        for t in range(tiles):
            cells = pl.ds((h * tiles + t) * LANES, LANES)
            halves_ref[pl.ds(h * own * tiles + t, own, stride=tiles), :] = field_ref[:, cells]


def start_kernel(tiles, right_ref, sent_ref, direct_ref):
    lay_kernel(tiles, right_ref, direct_ref)
    spread_out(direct_ref[...].astype(BF16), sent_ref)


def spread_out(both, sent_ref):
    devices, rows, _ = sent_ref.shape
    low, high = both[:rows], both[rows:]
    for chip in range(devices // 2):
        sent_ref[2 * chip] = low
        sent_ref[2 * chip + 1] = high


def load_kernel(
    tiles, ens_hbm, nbr_hbm, weight_hbm, obs_hbm, mine_ref, ens_ref, share_ref, acc_ref, obs_ref, mine,
    held, nbr_ref, weight_ref, laid, sems, small,
):
    members, blocks, cells = ens_hbm.shape
    half = cells // 2
    core = core_index()
    each = sems.shape[1]
    chunks, each = each, members // each

    def copies(c):
        span = pl.ds(c * each, each)
        out = []
        for slot in range(2):
            col = pl.multiple_of(lax.rem(core + slot, 2) * half, half)
            source = ens_hbm.at[span, :, pl.ds(col, half)]
            out.append(pltpu.make_async_copy(source, held.at[slot, span], sems.at[slot, c]))
        return out

    lists = (
        pltpu.make_async_copy(nbr_hbm, nbr_ref, small.at[0]),
        pltpu.make_async_copy(weight_hbm, weight_ref, small.at[1]),
        pltpu.make_async_copy(obs_hbm, laid, small.at[2]),
    )
    for copy in lists:
        copy.start()

    def begin(c, _):
        for copy in copies(c):
            copy.start()
        return 0

    lax.fori_loop(0, chunks, begin, 0)
    mine[...] = mine_ref[...].astype(F32)
    for copy in lists:
        copy.wait()
    lay_kernel(tiles, laid, obs_ref)
    away = nbr_ref[...] - lax.broadcasted_iota(jnp.int32, nbr_ref.shape, 1)
    away = jnp.where(away > blocks // 2, away - blocks, away)
    away = jnp.where(away < -(blocks // 2), away + blocks, away)
    row = lax.broadcasted_iota(jnp.int32, (8, blocks), 0)
    shares = jnp.zeros((8, blocks), F32)
    for i, shift in enumerate(SHIFTS):
        share = jnp.sum(jnp.where(away == shift, weight_ref[...], 0.0), axis=0, keepdims=True)
        shares = jnp.where(row == i, share, shares)
    shares = shares.T
    for i in range(len(SHIFTS)):
        share_ref[i] = jnp.broadcast_to(shares[:, i : i + 1], (blocks, LANES))

    acc_ref[...] = jnp.zeros_like(acc_ref)
    lane = lax.broadcasted_iota(jnp.int32, (ROWS, LANES), 1)

    def chunk(c, _):
        for copy in copies(c):
            copy.wait()

        def body(first):
            here = pl.ds(first, ROWS)
            parts = [every(mine, t, first, ROWS, tiles) for t in range(tiles)]
            sums = acc_ref[here, :]
            for i in range(each):
                k = c * each + i
                acc = None
                for t in range(tiles):
                    cells = pl.ds(t * LANES, LANES)
                    one = held[0, k, here, cells].astype(F32)
                    ens_ref[0, k, here, cells] = one
                    acc = one * parts[t] if acc is None else acc + one * parts[t]
                sums = jnp.where(lane == k, jnp.sum(acc, axis=1, keepdims=True), sums)
                for t in range(tiles):
                    cells = pl.ds(t * LANES, LANES)
                    ens_ref[1, k, here, cells] = held[1, k, here, cells].astype(F32)
            acc_ref[here, :] = sums

        groups(blocks, ROWS, 8, body)
        return 0

    lax.fori_loop(0, chunks, chunk, 0)


def groups(blocks, rows, unroll, body):
    def group(g, _):
        body(g * rows if isinstance(g, int) else pl.multiple_of(g * rows, rows))
        return 0

    lax.fori_loop(0, blocks // rows, group, 0, unroll=unroll)


def own_sums_kernel(tiles, ens_ref, mine_ref, dm_ref, do_ref, acc_ref, dd_ref, pd_ref, pp_ref, mine):
    blocks = ens_ref.shape[2]
    mine[...] = mine_ref[...].astype(F32)

    half_sums(ens_ref, 0, mine, acc_ref, tiles)

    def body(first):
        here = pl.ds(first, 8)
        parts = [every(mine, t, first, 8, tiles) for t in range(tiles)]
        own = [every(dm_ref, t, first, 8, tiles) for t in range(tiles)]
        far = [every(do_ref, t, first, 8, tiles) for t in range(tiles)]
        dd_ref[here, :] = sum(d * d for d in own + far)
        pd_ref[here, :] = sum(p * d for p, d in zip(parts, own))
        pp_ref[here, :] = sum(p * p for p in parts)

    groups(blocks, 8, 16, body)


def half_sums(ens_ref, slot, field, sums_ref, tiles, start=None):
    _, members, blocks, _ = ens_ref.shape
    lane = lax.broadcasted_iota(jnp.int32, (ROWS, LANES), 1)

    def body(first):
        here = pl.ds(first, ROWS)
        parts = [every(field, t, first, ROWS, tiles) for t in range(tiles)]
        out = jnp.zeros((ROWS, LANES), F32)
        for k in range(members):
            acc = None
            for t in range(tiles):
                term = ens_ref[slot, k, here, pl.ds(t * LANES, LANES)] * parts[t]
                acc = term if acc is None else acc + term
            out = jnp.where(lane == k, jnp.sum(acc, axis=1, keepdims=True), out)
        sums_ref[here, :] = out if start is None else out + start[here, :]

    groups(blocks, ROWS, 8, body)


def mixed(sums, pad_ref, share_ref):
    blocks = sums.shape[0]
    pad_ref[pl.ds(8, blocks), :] = sums
    pad_ref[pl.ds(0, 8), :] = sums[blocks - 8 :]
    pad_ref[pl.ds(8 + blocks, 8), :] = sums[:8]
    total = sums
    for i, shift in enumerate(SHIFTS):
        total = total + share_ref[i] * pad_ref[pl.ds(8 + shift, blocks), :]
    return total.astype(BF16).astype(F32)


def half_spread(ens_ref, slot, coeff, wide_ref, out_ref, tiles, send_ref=None):
    _, members, blocks, _ = ens_ref.shape
    rows, unroll = (8, 16) if coeff is None else (16, 8)

    def body(first):
        here = None if coeff is None else coeff[pl.ds(first, rows), :]
        acc = [None] * tiles
        for k in range(members):
            if here is None:
                one = wide_ref[k, pl.ds(first, rows), :]
            else:
                one = jnp.broadcast_to(here[:, k : k + 1].astype(BF16), (rows, LANES)).astype(F32)
                wide_ref[k, pl.ds(first, rows), :] = one
            for t in range(tiles):
                term = ens_ref[slot, k, pl.ds(first, rows), pl.ds(t * LANES, LANES)] * one
                acc[t] = term if acc[t] is None else acc[t] + term
        for t in range(tiles):
            out_ref[pl.ds(first * tiles + t, rows, stride=tiles), :] = acc[t]
        if send_ref is not None:
            span = pl.ds(first * tiles, rows * tiles)
            send_ref[span, :] = out_ref[span, :].astype(BF16)

    groups(blocks, rows, unroll, body)


def first_kernel(tiles, ens_ref, acc_ref, other_ref, share_ref, send_ref, sums_ref, wide_ref, other, pad_ref, coeff_ref, spread):
    other[...] = other_ref[...].astype(F32)
    half_sums(ens_ref, 1, other, sums_ref, tiles, acc_ref)
    coeff_ref[...] = mixed(sums_ref[...], pad_ref, share_ref)
    half_spread(ens_ref, 1, coeff_ref, wide_ref, spread, tiles, send_ref)


def own_kernel(tiles, ens_ref, wide_ref, own_ref):
    half_spread(ens_ref, 0, None, wide_ref, own_ref, tiles)


def received(got, rows):
    devices = got.shape[0]
    sums = []
    for core in range(2):
        total = None
        for chip in range(devices // 2):
            one = got[2 * chip + core, :rows, :].astype(F32)
            total = one if total is None else total + one
        sums.append(total)
    return jnp.concatenate(sums, axis=0)


def middle_kernel(tiles, got_ref, direct_ref, obs_ref, q_ref, sent_ref):
    _, rows, _ = got_ref.shape
    direct = direct_ref[...]
    q = obs_ref[...] * direct + received(got_ref, rows) * (1.0 / M)
    q_ref[...] = q
    d = direct.astype(BF16).astype(F32)
    dd = jnp.sum(direct * d, axis=1, keepdims=True)
    qd = jnp.sum(d * q, axis=1, keepdims=True)
    row = lax.broadcasted_iota(jnp.int32, dd.shape, 0) % rows // tiles
    tau = jnp.zeros_like(dd)
    for b in range(rows // tiles):
        here = row == b
        self = jnp.sum(jnp.where(here, dd, 0.0), axis=0, keepdims=True)
        prod = jnp.sum(jnp.where(here, qd, 0.0), axis=0, keepdims=True)
        share = jnp.where(self > 0.0, (1.0 - KEEP) * prod / jnp.where(self > 0.0, self, 1.0), 0.0)
        tau = jnp.where(here, share, tau)
    spread_out((q - tau * direct).astype(BF16), sent_ref)


def second_kernel(
    tiles, ens_ref, acc_ref, dd_ref, pd_ref, pp_ref, do_ref, po_ref, share_ref, sums0_ref,
    send_ref, wide_ref, scal_ref, sums_ref, coeff_ref, other, pd_all, pp_all, pad_ref, spread,
):
    blocks = ens_ref.shape[2]
    other[...] = po_ref[...].astype(F32)

    def products(first):
        here = pl.ds(first, ROWS)
        parts = [every(other, t, first, ROWS, tiles) for t in range(tiles)]
        far = [every(do_ref, t, first, ROWS, tiles) for t in range(tiles)]
        pd_all[here, :] = pd_ref[here, :] + sum(p * d for p, d in zip(parts, far))
        pp_all[here, :] = pp_ref[here, :] + sum(p * p for p in parts)

    groups(blocks, ROWS, 8, products)
    dd = jnp.sum(dd_ref[...], axis=1, keepdims=True)
    pd = jnp.sum(pd_all[...], axis=1, keepdims=True)
    pp = jnp.sum(pp_all[...], axis=1, keepdims=True)
    half_sums(ens_ref, 1, other, sums_ref, tiles, acc_ref)
    tau = jnp.where(dd > 0.0, (1.0 / KEEP - 1.0) * pd / jnp.where(dd > 0.0, dd, 1.0), 0.0)
    rr0 = jnp.sum(dd, axis=0, keepdims=True)
    alpha = rr0 / jnp.sum(pd + tau * dd, axis=0, keepdims=True)
    keep = 1.0 - alpha * tau
    rr1 = jnp.sum(keep * (keep * dd - 2.0 * alpha * pd) + alpha * alpha * pp, axis=0, keepdims=True)
    beta = rr1 / rr0
    row = lax.broadcasted_iota(jnp.int32, (8, LANES), 0)
    scal_ref[...] = jnp.where(row == 0, alpha, jnp.where(row == 1, beta, rr1))
    sums = (beta + keep) * sums0_ref[...] - alpha * sums_ref[...]
    sums_ref[...] = sums
    coeff_ref[...] = mixed(sums, pad_ref, share_ref)
    half_spread(ens_ref, 1, coeff_ref, wide_ref, spread, tiles, send_ref)


def second_own_kernel(
    tiles, ens_ref, wide_ref, sums_ref, coeff_ref, scal_ref, direct_ref, q_ref, obs_ref, own_ref, extra_ref
):
    alpha, beta = scal_ref[0:1, :], scal_ref[1:2, :]
    direction = (1.0 + beta) * direct_ref[...] - alpha * q_ref[...]
    part = jnp.sum(jnp.sum(sums_ref[...] * coeff_ref[...], axis=0, keepdims=True), axis=1, keepdims=True) * (1.0 / M)
    part += jnp.sum(jnp.sum(obs_ref[...] * direction * direction, axis=0, keepdims=True), axis=1, keepdims=True)
    row = lax.broadcasted_iota(jnp.int32, (8, LANES), 0)
    lane = lax.broadcasted_iota(jnp.int32, (8, LANES), 1)
    high = part.astype(BF16).astype(F32)
    mid = (part - high).astype(BF16).astype(F32)
    extra_ref[...] = jnp.where(row == 0, jnp.where(lane < LANES // 2, high, mid), part - high - mid)
    half_spread(ens_ref, 0, None, wide_ref, own_ref, tiles)


def last_kernel(tiles, spread_ref, extra_ref, scal_ref, direct_ref, obs_ref, q_ref, solution_ref, residual_ref, sol, res):
    rows = spread_ref.shape[0] // 2
    parts = extra_ref[0] + extra_ref[1]
    denom = jnp.sum(parts[0:1], axis=1, keepdims=True) * (2.0 / LANES) + parts[1:2]
    alpha, beta, rr1 = scal_ref[0:1, :], scal_ref[1:2, :], scal_ref[2:3, :]
    direct = direct_ref[...]
    residual = direct - alpha * q_ref[...]
    direction = residual + beta * direct
    image = obs_ref[...] * direction + spread_ref[...] * (1.0 / M)
    alpha1 = rr1 / denom
    sol[...] = alpha * direct + alpha1 * direction
    res[...] = residual - alpha1 * image
    own = solution_ref.shape[0]
    for h in range(2):
        for t in range(tiles):
            cells = pl.ds((h * tiles + t) * LANES, LANES)
            at = pl.ds(h * rows + t, own, stride=tiles)
            solution_ref[:, cells] = sol[at, :]
            residual_ref[:, cells] = res[at, :]


def call(kernel, name, outs, ins, scratch=(), mib=8, cost=(0, 0)):
    return pl.pallas_call(
        kernel,
        name=name,
        out_shape=tuple(outs),
        in_specs=ins,
        out_specs=(VMEM,) * len(outs),
        scratch_shapes=list(scratch),
        compiler_params=pltpu.CompilerParams(vmem_limit_bytes=mib * 1024 * 1024),
        cost_estimate=pl.CostEstimate(flops=cost[0], bytes_accessed=cost[1], transcendentals=0),
    )


def per_device(ensemble, right_side, obs_prec, neighbors, loc_weight):
    own, cells = right_side.shape
    members, blocks, _ = ensemble.shape
    devices = lax.axis_size(AXES)
    tiles = cells // (2 * LANES)
    rows = own * tiles
    half = blocks * tiles
    pairs = [(i, i ^ 1) for i in range(devices)]
    shape = jax.ShapeDtypeStruct
    part = functools.partial
    mib = 4 + 4 * blocks // 128

    def swap(x):
        return lax.ppermute(x, AXES, pairs)

    def exchange(x):
        return lax.all_to_all(x, AXES, split_axis=0, concat_axis=0, tiled=True)

    to_all = shape((devices, rows, LANES), BF16)
    lanes = shape((members, blocks, LANES), F32)
    table = shape((blocks, LANES), F32)
    to_swap = shape((half, LANES), BF16)
    part_half = shape((half, LANES), F32)
    mine = shape((2 * rows, LANES), F32)
    field = pltpu.VMEM((half, LANES), F32)
    padded = pltpu.VMEM((blocks + 16, LANES), F32)
    work = 2 * members * blocks * cells

    sent, direct = call(part(start_kernel, tiles), "start", (to_all, mine), [VMEM])(right_side)
    d_mine = exchange(sent).reshape(half, LANES)
    d_other = swap(d_mine)
    ens, share, acc, obs, d_mine = call(
        part(load_kernel, tiles),
        "load",
        (shape((2, members, blocks, cells // 2), F32), shape((len(SHIFTS), blocks, LANES), F32), table, mine, part_half),
        [HBM, HBM, HBM, HBM, VMEM],
        [
            pltpu.VMEM((2, members, blocks, cells // 2), BF16),
            pltpu.VMEM(neighbors.shape[::-1], jnp.int32),
            pltpu.VMEM(loc_weight.shape[::-1], F32),
            pltpu.VMEM((own, cells), F32),
            pltpu.SemaphoreType.DMA((2, members // 4)),
            pltpu.SemaphoreType.DMA((3,)),
        ],
        mib=8 + mib,
        cost=(work, 6 * members * blocks * cells),
    )(*(pltpu.with_memory_space_constraint(x, pltpu.HBM) for x in (ensemble, neighbors.T, loc_weight.T, obs_prec)), d_mine)

    coeffs = pltpu.VMEM((blocks, LANES), F32)
    send, sums0, wide, d_other = call(
        part(first_kernel, tiles), "first", (to_swap, table, lanes, part_half), [VMEM] * 4, [padded, coeffs, field],
        mib=mib, cost=(work, 0),
    )(ens, acc, d_other, share)
    (kept,) = call(part(own_kernel, tiles), "own", (part_half,), [VMEM] * 2, mib=mib, cost=(work, 0))(ens, wide)
    got = exchange((kept + swap(send).astype(F32)).astype(BF16).reshape(to_all.shape))

    q, sent = call(part(middle_kernel, tiles), "middle", (mine, to_all), [VMEM] * 3)(got, direct, obs)
    p_mine = exchange(sent).reshape(half, LANES)
    p_other = swap(p_mine)

    small = shape((8, LANES), F32)
    acc, dd, pd, pp = call(
        part(own_sums_kernel, tiles), "sums", (table, table, table, table), [VMEM] * 4, [field], mib=mib, cost=(work, 0)
    )(ens, p_mine, d_mine, d_other)
    send, wide, scal, sums, coeff = call(
        part(second_kernel, tiles),
        "second",
        (to_swap, lanes, small, table, table),
        [VMEM] * 9,
        [field, coeffs, coeffs, padded, field],
        mib=mib,
        cost=(work, 0),
    )(ens, acc, dd, pd, pp, d_other, p_other, share, sums0)
    kept, extra = call(
        part(second_own_kernel, tiles), "second_own", (part_half, small), [VMEM] * 8, mib=mib, cost=(work, 0)
    )(ens, wide, sums, coeff, scal, direct, q, obs)
    both = (kept + swap(send).astype(F32)).astype(BF16).reshape(devices, rows // 2, 2, LANES)
    extra = jnp.broadcast_to(extra[:2].astype(BF16).reshape(1, 1, 2, LANES), (devices, 1, 2, LANES))
    got = exchange(jnp.concatenate([both, extra], axis=1))
    got = jnp.sum(got.reshape(devices // 2, 2, rows // 2 + 1, 2, LANES).astype(F32), axis=0)
    spread = got[:, : rows // 2].reshape(2 * rows, LANES)
    extra = got[:, rows // 2]
    out = shape((own, cells), F32)
    scratch = pltpu.VMEM((2 * rows, LANES), F32)
    return call(part(last_kernel, tiles), "last", (out, out), [VMEM] * 6, [scratch] * 2)(spread, extra, scal, direct, obs, q)


def solution(mesh):
    return jax.shard_map(
        per_device,
        mesh=mesh,
        in_specs=(
            P(AXES, None, None),
            P(AXES, None),
            P(AXES, None),
            P(),
            P(),
        ),
        out_specs=(P(AXES, None), P(AXES, None)),
        check_vma=False,
    )
```
